256 devices in a mesh: gz: 32 (over y_lo, z, core), gy: 8 (over x, y_hi).
Axes of the slice: x: 4, y: 4 (y_hi: 2, y_lo: 2; y = y_hi * 2 + y_lo), z: 8, core: 2. Of those that a mesh axis runs over, the one named last changes fastest.
Arguments:
- potential: float32 [256, 512, 512], P('gz', 'gy'), may hold values from 0 to 1
- fast_gate: float32 [256, 512, 512], P('gz', 'gy'), may hold values from 0 to 1
- slow_gate: float32 [256, 512, 512], P('gz', 'gy'), may hold values from 0 to 1
- tissue: int32 [256, 512, 512], P('gz', 'gy'), may hold values 0 or 1
- region_ids: int32 [32, 64, 64], P('gz', 'gy'), may hold values from 0 to 7
- fibre_table: float32 [8, 3], replicated, may hold values from -1 to 1
- inverse_x: float32 [512, 512], replicated, may hold values from -1 to 1
- inverse_z: float32 [256, 256], replicated, may hold values from -1 to 1
- inverse_y: float32 [512, 512], replicated, may hold values from -1 to 1
Outputs:
- new_potential: float32 [256, 512, 512], P('gz', 'gy')
- new_fast: float32 [256, 512, 512], P('gz', 'gy')
- new_slow: float32 [256, 512, 512], P('gz', 'gy')
The draws below stay inside these ranges and needn't reach their ends.
All inputs are finite; a program needn't handle non-finite values. No bound on the sum of `tissue` on one device may be relied on, other than what follows from the above.
Results may differ from the reference program's by a relative error of at most 0.0003.
Values sent between devices are 32-bit elements; how exact they have to be, the bound alone decides.
No kernel may reach another device: no remote copies, remote signals or barrier semaphores. Data moves between devices by JAX's collectives and lax.ppermute only.
A program may use at most 64 MiB of HBM per device.

```python
import jax
import jax.numpy as jnp
from jax import lax

NX = 512
REGIONS = 8
NY = 512
NZ = 256


def inverse_matrix(key, order):
    noise_key, diag_key = jax.random.split(key)
    rows = jnp.arange(order)[:, None]
    cols = jnp.arange(order)[None, :]
    distance = jnp.abs(rows - cols).astype(jnp.float32)
    noise = jax.random.normal(noise_key, (order, order), jnp.float32)
    diagonal = jax.random.uniform(diag_key, (order,), jnp.float32, 0.4, 0.8)
    spread = jnp.exp(-distance / (order / 4.0)) * (1.0 + 0.5 * noise) / order
    return jnp.eye(order, dtype=jnp.float32) * diagonal[:, None] + spread


def draw_inverse_x(key, part):
    key = jax.random.fold_in(key, 11)
    return inverse_matrix(key, NX)


def draw_inverse_z(key, part):
    key = jax.random.fold_in(key, 12)
    return inverse_matrix(key, NZ)


def draw_inverse_y(key, part):
    key = jax.random.fold_in(key, 13)
    return inverse_matrix(key, NY)


def with_ends(drawn, rng, least, high):
    extent = drawn.shape
    index_at = [jax.random.randint(jax.random.fold_in(rng, axis), (), 0, extent[axis]) for axis in range(len(extent))]
    drawn = drawn.at[tuple(index_at)].set(least)
    longest = extent.index(max(extent))
    index_at[longest] = (index_at[longest] + 1) % extent[longest]
    return drawn.at[tuple(index_at)].set(high)


def block_levels(key, dims, cuts, smallest, largest):
    level = 1.0
    for position, blocks in cuts:
        heights = jax.random.uniform(jax.random.fold_in(jax.random.fold_in(key, 6), position), (blocks,), jnp.float32, smallest / len(cuts), largest / len(cuts))
        level = level * jnp.repeat(jnp.exp(heights), dims[position] // blocks).reshape((-1,) + (1,) * (len(dims) - 1 - position))
    return level


def setup_inputs(seed: int = 0) -> dict:
    seeds = jax.random.split(jax.random.key(seed), 10)
    potential = jnp.clip(1.0 * jax.random.uniform(seeds[0], (NZ, NY, NX), jnp.float32) ** block_levels(seeds[0], (NZ, NY, NX), ((0, 32), (1, 8)), -0.2, 0.2), 0.0, 1.0)
    fast_gate = jnp.clip(1.0 * jax.random.uniform(seeds[1], (NZ, NY, NX), jnp.float32) ** block_levels(seeds[1], (NZ, NY, NX), ((0, 32), (1, 8)), -0.2, 0.2), 0.0, 1.0)
    slow_gate = jnp.clip(1.0 * jax.random.uniform(seeds[2], (NZ, NY, NX), jnp.float32) ** block_levels(seeds[2], (NZ, NY, NX), ((0, 32), (1, 8)), -0.2, 0.2), 0.0, 1.0)
    tissue = with_ends((jax.random.randint(seeds[3], (NZ, NY, NX), 0, 10) < 9).astype(jnp.int32), jax.random.fold_in(seeds[3], 1), 0, 1)
    region_ids = with_ends(jax.random.randint(seeds[4], (NZ // 8, NY // 8, NX // 8), 0, REGIONS), jax.random.fold_in(seeds[4], 1), 0, REGIONS - 1).astype(jnp.int32)
    fibre_table = jnp.clip(jax.random.uniform(seeds[5], (REGIONS, 3), jnp.float32, -1.0, 1.0), -1.0, 1.0)
    inverse_x = draw_inverse_x(jax.random.fold_in(seeds[9], 71), 0)
    inverse_z = draw_inverse_z(jax.random.fold_in(seeds[9], 71), 0)
    inverse_y = draw_inverse_y(jax.random.fold_in(seeds[9], 71), 0)
    return {"potential": potential, "fast_gate": fast_gate, "slow_gate": slow_gate, "tissue": tissue, "region_ids": region_ids, "fibre_table": fibre_table, "inverse_x": inverse_x, "inverse_z": inverse_z, "inverse_y": inverse_y}


time_step = 0.1
depol_tau = 0.25
repol_tau = 33.33
inward_tau = 29.0
outward_tau = 12.5
vclose_tau = 3.33
vopen_high = 19.6
vopen_low = 1250.0
wclose_tau = 870.0
wopen_tau = 41.0
gate_crit = 0.13
vgate_crit = 0.04
inward_crit = 0.85
inward_slope = 10.0


def ionic(potential, fast_gate, slow_gate, tissue):
    active = potential >= gate_crit
    current = jnp.where(active, -fast_gate * (1.0 - potential) * (potential - gate_crit) / depol_tau, 0.0)
    current = current + jnp.where(active, 1.0 / repol_tau, potential / outward_tau)
    current = current - slow_gate * (1.0 + jnp.tanh(inward_slope * (potential - inward_crit))) / (2.0 * inward_tau)
    excited = potential - time_step * current
    target = jnp.where(active, 0.0, 1.0)
    tau_fast = jnp.where(active, vclose_tau, jnp.where(potential >= vgate_crit, vopen_high, vopen_low))
    tau_slow = jnp.where(active, wclose_tau, wopen_tau)
    new_fast = target + (fast_gate - target) * jnp.exp(-time_step / tau_fast)
    new_slow = target + (slow_gate - target) * jnp.exp(-time_step / tau_slow)
    living = tissue == 1
    return (jnp.where(living, excited, potential), jnp.where(living, new_fast, fast_gate),
            jnp.where(living, new_slow, slow_gate))


def couplings(region_ids, fibre_table):
    picks = (region_ids[..., None] == jnp.arange(fibre_table.shape[0], dtype=jnp.int32)).astype(jnp.float32)
    return [jnp.sum(picks * fibre_table[:, column], axis=-1) for column in range(3)]


def blockwise(field, weight):
    za, ya, xa = weight.shape
    shaped = field.reshape(za, 8, ya, 8, xa, 8)
    return (shaped * weight[:, None, :, None, :, None]).reshape(field.shape)


def cross_term(padded, region_ids, fibre_table):
    mixed_xy = (padded[1:-1, 2:, 2:] - padded[1:-1, 2:, :-2] - padded[1:-1, :-2, 2:] + padded[1:-1, :-2, :-2]) / 4.0
    mixed_xz = (padded[2:, 1:-1, 2:] - padded[2:, 1:-1, :-2] - padded[:-2, 1:-1, 2:] + padded[:-2, 1:-1, :-2]) / 4.0
    mixed_yz = (padded[2:, 2:, 1:-1] - padded[2:, :-2, 1:-1] - padded[:-2, 2:, 1:-1] + padded[:-2, :-2, 1:-1]) / 4.0
    coef_xy, coef_xz, coef_yz = couplings(region_ids, fibre_table)
    total = blockwise(mixed_xy, coef_xy) + blockwise(mixed_xz, coef_xz) + blockwise(mixed_yz, coef_yz)
    return 2.0 * total


def reference(potential, fast_gate, slow_gate, tissue, region_ids, fibre_table, inverse_x, inverse_z, inverse_y):
    excited, new_fast, new_slow = ionic(potential, fast_gate, slow_gate, tissue)
    padded = jnp.pad(potential, 1)
    rhs = excited + cross_term(padded, region_ids, fibre_table)
    along_x = jnp.einsum('zyj,ij->zyi', rhs, inverse_x, precision=lax.Precision.HIGHEST)
    along_z = jnp.einsum('ij,jyx->iyx', inverse_z, along_x, precision=lax.Precision.HIGHEST)
    new_potential = jnp.einsum('ij,zjx->zix', inverse_y, along_z, precision=lax.Precision.HIGHEST)
    return new_potential, new_fast, new_slow
```

```python
import math

import jax
import jax.numpy as jnp
from jax import lax
from jax.experimental import pallas as pl
from jax.experimental.pallas import tpu as pltpu
from jax.sharding import PartitionSpec as P

time_step = 0.1
depol_tau = 0.25
repol_tau = 33.33
inward_tau = 29.0
outward_tau = 12.5
vclose_tau = 3.33
vopen_high = 19.6
vopen_low = 1250.0
wclose_tau = 870.0
wopen_tau = 41.0
gate_crit = 0.13
vgate_crit = 0.04
inward_crit = 0.85
inward_slope = 10.0

VMEM = pl.BlockSpec(memory_space=pltpu.VMEM)
SMEM = pl.BlockSpec(memory_space=pltpu.SMEM)
NT = (((1,), (1,)), ((), ()))
NN = (((1,), (0,)), ((), ()))


def decay(tau):
    return math.exp(-time_step / tau)


def split(values):
    high = values.astype(jnp.bfloat16)
    return high, (values - high.astype(jnp.float32)).astype(jnp.bfloat16)


def product(left, right, dims):
    (lh, ll), (rh, rl) = left, right

    def dot(a, b):
        return lax.dot_general(a, b, dims, preferred_element_type=jnp.float32)

    return dot(lh, rh) + (dot(lh, rl) + dot(ll, rh))


def ionic_kernel(pot_ref, fast_ref, slow_ref, tissue_ref, exc_ref, nfast_ref, nslow_ref):
    p, v, w = pot_ref[...], fast_ref[...], slow_ref[...]
    living = tissue_ref[...] == 1
    active = p >= gate_crit
    current = jnp.where(
        active,
        (1.0 / repol_tau) - v * (1.0 - p) * (p - gate_crit) * (1.0 / depol_tau),
        p * (1.0 / outward_tau),
    )
    current = current - w * (1.0 + jnp.tanh(inward_slope * (p - inward_crit))) * (
        1.0 / (2.0 * inward_tau)
    )
    exc_ref[...] = jnp.where(living, p - time_step * current, p)
    target = jnp.where(active, 0.0, 1.0)
    keep_fast = jnp.where(
        active, decay(vclose_tau), jnp.where(p >= vgate_crit, decay(vopen_high), decay(vopen_low))
    )
    keep_slow = jnp.where(active, decay(wclose_tau), decay(wopen_tau))
    nfast_ref[...] = jnp.where(living, target + (v - target) * keep_fast, v)
    nslow_ref[...] = jnp.where(living, target + (w - target) * keep_slow, w)


def ionic(potential, fast_gate, slow_gate, tissue):
    nz, ny, nx = potential.shape
    block = pl.BlockSpec((1, ny, nx), lambda z: (z, 0, 0))
    shape = jax.ShapeDtypeStruct((nz, ny, nx), jnp.float32)
    return pl.pallas_call(
        ionic_kernel,
        grid=(nz,),
        in_specs=[block] * 4,
        out_specs=[block] * 3,
        out_shape=[shape] * 3,
        cost_estimate=pl.CostEstimate(
            flops=40 * nz * ny * nx, bytes_accessed=28 * nz * ny * nx, transcendentals=0
        ),
        name="ionic",
    )(potential, fast_gate, slow_gate, tissue)


def lane_difference(values):
    width = values.shape[-1]
    lane = lax.broadcasted_iota(jnp.int32, values.shape, values.ndim - 1)
    ahead = pltpu.roll(values, width - 1, values.ndim - 1)
    behind = pltpu.roll(values, 1, values.ndim - 1)
    return jnp.where(lane == width - 1, 0.0, ahead) - jnp.where(lane == 0, 0.0, behind)


def cross_kernel(
    table_ref, pot_ref, exc_ref, zlo_ref, zhi_ref, ylo_ref, yhi_ref, region_ref, inv_ref,
    out_ref, pad_ref, dy_ref, coef_ref, high_ref, low_ref,
):
    nz, ny, nx = pot_ref.shape
    blocks = nx // 8
    regions = table_ref.shape[0]
    spread = (
        lax.broadcasted_iota(jnp.int32, (blocks, nx), 1) // 8
        == lax.broadcasted_iota(jnp.int32, (blocks, nx), 0)
    ).astype(jnp.bfloat16)
    ids = lax.dot_general(
        region_ref[...].astype(jnp.float32).astype(jnp.bfloat16), spread, NN,
        preferred_element_type=jnp.float32,
    )
    for column in range(3):
        coef = jnp.zeros_like(ids)
        for region in range(regions):
            coef = jnp.where(ids == float(region), 0.5 * table_ref[region, column], coef)
        coef_ref[column] = coef

    for z in range(nz + 2):
        plane = zlo_ref[...] if z == 0 else zhi_ref[...] if z == nz + 1 else pot_ref[z - 1]
        pad_ref[z, 8 : 8 + ny] = plane
        pad_ref[z, 7:8] = ylo_ref[z : z + 1]
        pad_ref[z, 8 + ny : 9 + ny] = yhi_ref[z : z + 1]
        dy_ref[z] = pad_ref[z, 9 : 9 + ny] - pad_ref[z, 7 : 7 + ny]

    for z in range(nz):
        mixed_xy = lane_difference(dy_ref[z + 1])
        mixed_xz = lane_difference(pad_ref[z + 2, 8 : 8 + ny] - pad_ref[z, 8 : 8 + ny])
        mixed_yz = dy_ref[z + 2] - dy_ref[z]
        for b in range(ny // 8):
            rows = slice(8 * b, 8 * b + 8)
            rhs = exc_ref[z, rows] + (
                coef_ref[0, b : b + 1] * mixed_xy[rows]
                + coef_ref[1, b : b + 1] * mixed_xz[rows]
                + coef_ref[2, b : b + 1] * mixed_yz[rows]
            )
            pad_ref[0, rows] = rhs
        high, low = split(pad_ref[0, 0:ny])
        high_ref[z * ny : (z + 1) * ny] = high
        low_ref[z * ny : (z + 1) * ny] = low

    half = nx // 2
    matrix = split(inv_ref[...])
    first = lax.broadcasted_iota(jnp.int32, (half, 2 * ny), 1) < ny
    for z in range(0, nz, 2):
        rows = slice(z * ny, (z + 2) * ny)
        solved = product(matrix, (high_ref[rows], low_ref[rows]), NT)
        lower, upper = solved[:half], solved[half:]
        out_ref[:, z, :] = jnp.where(first, lower, pltpu.roll(upper, ny, 1))
        out_ref[:, z + 1, :] = jnp.where(first, pltpu.roll(lower, ny, 1), upper)


def cross_solve(table, potential, excited, zlo, zhi, ylo, yhi, region, inverse_x):
    nz, ny, nx = potential.shape
    return pl.pallas_call(
        cross_kernel,
        in_specs=[SMEM] + [VMEM] * 8,
        out_specs=VMEM,
        out_shape=jax.ShapeDtypeStruct((nx // 2, nz, 2 * ny), jnp.float32),
        scratch_shapes=[
            pltpu.VMEM((nz + 2, ny + 16, nx), jnp.float32),
            pltpu.VMEM((nz + 2, ny, nx), jnp.float32),
            pltpu.VMEM((3, ny // 8, nx), jnp.float32),
            pltpu.VMEM((nz * ny, nx), jnp.bfloat16),
            pltpu.VMEM((nz * ny, nx), jnp.bfloat16),
        ],
        compiler_params=pltpu.CompilerParams(vmem_limit_bytes=40 * 1024 * 1024),
        cost_estimate=pl.CostEstimate(
            flops=6 * nz * ny * nx * nx, bytes_accessed=16 * nz * ny * nx, transcendentals=0
        ),
        name="cross_solve",
    )(table, potential, excited, zlo, zhi, ylo, yhi, region, inverse_x)


def plane_kernel(in_ref, invz_ref, invy_ref, out_ref, high_ref, low_ref):
    slabs, blocks, depth, width = in_ref.shape
    half = width // 2
    rows = slabs * depth
    matz, maty = split(invz_ref[...]), split(invy_ref[...])
    first = lax.broadcasted_iota(jnp.int32, (rows, width), 1) < half
    for b in range(0, blocks, 2):
        pair = []
        for k in (b, b + 1):
            pair.append(in_ref[:, k].reshape(rows, width))
        solved = product(matz, split(jnp.concatenate(pair, axis=1)), NN)
        left, right = solved[:, :width], solved[:, width:]
        columns = slice(b * half, (b + 2) * half)
        high_ref[:rows, columns], low_ref[:rows, columns] = split(
            jnp.where(first, left, pltpu.roll(right, half, 1))
        )
        high_ref[rows:, columns], low_ref[rows:, columns] = split(
            jnp.where(first, pltpu.roll(left, half, 1), right)
        )
    for b in range(0, blocks, 2):
        columns = slice(b * half, (b + 2) * half)
        solved = product(
            (high_ref[...], low_ref[...]), (maty[0][columns], maty[1][columns]), NT
        )
        one, two = solved[:rows], solved[rows:]
        out_ref[:, b] = jnp.where(first, one, pltpu.roll(two, half, 1)).reshape(slabs, depth, width)
        out_ref[:, b + 1] = jnp.where(first, pltpu.roll(one, half, 1), two).reshape(
            slabs, depth, width
        )


def plane_solve(planes, inverse_z, inverse_y):
    slabs, blocks, depth, width = planes.shape
    nz, ny = inverse_z.shape[0], inverse_y.shape[0]
    return pl.pallas_call(
        plane_kernel,
        in_specs=[VMEM] * 3,
        out_specs=VMEM,
        out_shape=jax.ShapeDtypeStruct(planes.shape, jnp.float32),
        scratch_shapes=[pltpu.VMEM((2 * nz, ny), jnp.bfloat16)] * 2,
        compiler_params=pltpu.CompilerParams(vmem_limit_bytes=40 * 1024 * 1024),
        cost_estimate=pl.CostEstimate(
            flops=12 * nz * ny * (nz + ny), bytes_accessed=16 * nz * ny, transcendentals=0
        ),
        name="plane_solve",
    )(planes, inverse_z, inverse_y)


def unpack_kernel(in_ref, out_ref):
    sources, depth, width = in_ref.shape
    ny = width // 2
    for z in range(depth):
        turned = in_ref[:, z, :].T
        out_ref[z, :, :sources] = turned[:ny]
        out_ref[z, :, sources:] = turned[ny:]


def unpack(tiles):
    sources, depth, width = tiles.shape
    return pl.pallas_call(
        unpack_kernel,
        in_specs=[VMEM],
        out_specs=VMEM,
        out_shape=jax.ShapeDtypeStruct((depth, width // 2, 2 * sources), jnp.float32),
        cost_estimate=pl.CostEstimate(
            flops=0, bytes_accessed=8 * sources * depth * width, transcendentals=0
        ),
        name="unpack",
    )(tiles)


def edges(values, axis):
    count = lax.axis_size(axis)
    up = [(i, i + 1) for i in range(count - 1)]
    down = [(i + 1, i) for i in range(count - 1)]
    head, tail = values
    return lax.ppermute(tail, axis, up), lax.ppermute(head, axis, down)


def shards(
    potential,
    fast_gate,
    slow_gate,
    tissue,
    region_ids,
    fibre_table,
    inverse_x,
    inverse_z,
    inverse_y,
):
    zlo, zhi = edges((potential[0], potential[-1]), "gz")
    rows_lo = jnp.concatenate([zlo[:1], potential[:, 0], zhi[:1]], axis=0)
    rows_hi = jnp.concatenate([zlo[-1:], potential[:, -1], zhi[-1:]], axis=0)
    ylo, yhi = edges((rows_lo, rows_hi), "gy")
    excited, new_fast, new_slow = ionic(potential, fast_gate, slow_gate, tissue)
    tiles = cross_solve(
        fibre_table, potential, excited, zlo, zhi, ylo, yhi, region_ids[0], inverse_x
    )
    axes = ("gz", "gy")
    planes = lax.all_to_all(tiles, axes, split_axis=0, concat_axis=0, tiled=True)
    slabs, blocks = lax.axis_size("gz"), lax.axis_size("gy")
    solved = plane_solve(planes.reshape((slabs, blocks) + planes.shape[1:]), inverse_z, inverse_y)
    back = lax.all_to_all(
        solved.reshape(planes.shape), axes, split_axis=0, concat_axis=0, tiled=True
    )
    return (unpack(back), new_fast, new_slow)


def solution(mesh):
    return jax.shard_map(
        shards,
        mesh=mesh,
        in_specs=(
            P("gz", "gy", None),
            P("gz", "gy", None),
            P("gz", "gy", None),
            P("gz", "gy", None),
            P("gz", "gy", None),
            P(),
            P(),
            P(),
            P(),
        ),
        out_specs=(P("gz", "gy", None), P("gz", "gy", None), P("gz", "gy", None)),
        check_vma=False,
    )
```

```python
import math

import jax
import jax.numpy as jnp
from jax import lax
from jax.experimental import pallas as pl
from jax.experimental.pallas import tpu as pltpu
from jax.sharding import PartitionSpec as P

time_step = 0.1
depol_tau = 0.25
repol_tau = 33.33
inward_tau = 29.0
outward_tau = 12.5
vclose_tau = 3.33
vopen_high = 19.6
vopen_low = 1250.0
wclose_tau = 870.0
wopen_tau = 41.0
gate_crit = 0.13
vgate_crit = 0.04
inward_crit = 0.85
inward_slope = 10.0

VMEM = pl.BlockSpec(memory_space=pltpu.VMEM)
HBM = pl.BlockSpec(memory_space=pltpu.HBM)
SMEM = pl.BlockSpec(memory_space=pltpu.SMEM)
NT = (((1,), (1,)), ((), ()))
NN = (((1,), (0,)), ((), ()))


def decay(tau):
    return math.exp(-time_step / tau)


def split(values):
    high = values.astype(jnp.bfloat16)
    return high, (values - high.astype(jnp.float32)).astype(jnp.bfloat16)


def product(left, right, dims):
    (lh, ll), (rh, rl) = left, right

    def dot(a, b):
        return lax.dot_general(a, b, dims, preferred_element_type=jnp.float32)

    return dot(lh, rh) + (dot(lh, rl) + dot(ll, rh))


def ionic_kernel(
    pot_ref, fast_ref, slow_ref, tissue_ref,
    potc_ref, exc_ref, low_ref, high_ref, nfast_ref, nslow_ref,
    fast_v, slow_v, tissue_v, nfast_v, nslow_v, in_sems, out_sems,
):
    nz, ny, _ = pot_ref.shape
    pairs = ((pot_ref, potc_ref), (fast_ref, fast_v), (slow_ref, slow_v), (tissue_ref, tissue_v))
    loads = [
        [
            pltpu.make_async_copy(source.at[z], target.at[z], in_sems.at[k, z])
            for k, (source, target) in enumerate(pairs)
        ]
        for z in range(nz)
    ]
    stores = [
        [
            pltpu.make_async_copy(source.at[z], target.at[z], out_sems.at[k, z])
            for k, (source, target) in enumerate(((nfast_v, nfast_ref), (nslow_v, nslow_ref)))
        ]
        for z in range(nz)
    ]
    for group in loads:
        for copy in group:
            copy.start()
    for z in range(nz):
        for copy in loads[z]:
            copy.wait()
        low_ref[z : z + 1] = potc_ref[z, :1]
        high_ref[z : z + 1] = potc_ref[z, ny - 1 :]
        for row in range(0, ny, 8):
            rows = (z, slice(row, row + 8))
            p, v, w = potc_ref[rows], fast_v[rows], slow_v[rows]
            living = tissue_v[rows] == 1
            active = p >= gate_crit
            exc_ref[rows] = jnp.where(living, excite(p, v, w, active), p)
            target = jnp.where(active, 0.0, 1.0)
            keep_fast = jnp.where(
                active,
                decay(vclose_tau),
                jnp.where(p >= vgate_crit, decay(vopen_high), decay(vopen_low)),
            )
            keep_slow = jnp.where(active, decay(wclose_tau), decay(wopen_tau))
            nfast_v[rows] = jnp.where(living, target + (v - target) * keep_fast, v)
            nslow_v[rows] = jnp.where(living, target + (w - target) * keep_slow, w)
        for copy in stores[z]:
            copy.start()
    for group in stores:
        for copy in group:
            copy.wait()


def ionic(potential, fast_gate, slow_gate, tissue):
    nz, ny, nx = potential.shape
    shape = jax.ShapeDtypeStruct((nz, ny, nx), jnp.float32)
    line = pltpu.VMEM((nz, nx), jnp.float32)
    field = pltpu.VMEM((nz, ny, nx), jnp.float32)
    return pl.pallas_call(
        ionic_kernel,
        in_specs=[HBM] * 4,
        out_specs=[VMEM] * 4 + [HBM] * 2,
        out_shape=[field, field, line, line, shape, shape],
        scratch_shapes=[
            field,
            field,
            pltpu.VMEM((nz, ny, nx), jnp.int32),
            field,
            field,
            pltpu.SemaphoreType.DMA((4, nz)),
            pltpu.SemaphoreType.DMA((2, nz)),
        ],
        compiler_params=pltpu.CompilerParams(vmem_limit_bytes=32 * 1024 * 1024),
        cost_estimate=pl.CostEstimate(
            flops=40 * nz * ny * nx, bytes_accessed=24 * nz * ny * nx, transcendentals=0
        ),
        name="ionic",
    )(*(pltpu.with_memory_space_constraint(a, pltpu.HBM) for a in (potential, fast_gate, slow_gate, tissue)))


def excite(p, v, w, active):
    current = jnp.where(
        active,
        (1.0 / repol_tau) - v * (1.0 - p) * (p - gate_crit) * (1.0 / depol_tau),
        p * (1.0 / outward_tau),
    )
    current = current - w * (1.0 + jnp.tanh(inward_slope * (p - inward_crit))) * (
        1.0 / (2.0 * inward_tau)
    )
    return p - time_step * current


def lane_difference(values):
    width = values.shape[-1]
    lane = lax.broadcasted_iota(jnp.int32, values.shape, values.ndim - 1)
    ahead = pltpu.roll(values, width - 1, values.ndim - 1)
    behind = pltpu.roll(values, 1, values.ndim - 1)
    return jnp.where(lane == width - 1, 0.0, ahead) - jnp.where(lane == 0, 0.0, behind)


def coefficients(table_ref, region_ref, nx):
    blocks = region_ref.shape[1]
    spread = (
        lax.broadcasted_iota(jnp.int32, (blocks, nx), 1) // 8
        == lax.broadcasted_iota(jnp.int32, (blocks, nx), 0)
    ).astype(jnp.bfloat16)
    ids = lax.dot_general(
        region_ref[...].astype(jnp.float32).astype(jnp.bfloat16), spread, NN,
        preferred_element_type=jnp.float32,
    )
    coefs = []
    for column in range(3):
        coef = jnp.zeros_like(ids)
        for region in range(table_ref.shape[0]):
            coef = jnp.where(ids == float(region), 0.5 * table_ref[region, column], coef)
        coefs.append(coef)
    return coefs


def ordered(odd, inner, outer):
    return jnp.where(odd == 1, inner, outer), jnp.where(odd == 1, outer, inner)


def stencil_kernel(
    table_ref, pot_ref, exc_ref, inner_ref, outer_ref, region_ref, inv_ref,
    rhs_ref, coef_ref, ihigh_ref, ilow_ref, pad_ref, dy_ref,
):
    nz, ny, nx = pot_ref.shape
    for column, coef in enumerate(coefficients(table_ref, region_ref, nx)):
        coef_ref[column] = coef
    below, above = ordered(lax.axis_index("gz") % 2, inner_ref[...], outer_ref[...])
    nothing = jnp.zeros((1, nx), jnp.float32)
    for z in range(nz + 2):
        plane = below if z == 0 else above if z == nz + 1 else pot_ref[z - 1]
        pad_ref[z, 8 : 8 + ny] = plane
        pad_ref[z, 7:8] = nothing
        pad_ref[z, 8 + ny : 9 + ny] = nothing
        dy_ref[z] = pad_ref[z, 9 : 9 + ny] - pad_ref[z, 7 : 7 + ny]
    for z in range(nz):
        for b in range(ny // 8):
            rows = slice(8 * b, 8 * b + 8)
            inside = slice(8 * b + 8, 8 * b + 16)
            mixed_xy = lane_difference(dy_ref[z + 1, rows])
            mixed_xz = lane_difference(pad_ref[z + 2, inside] - pad_ref[z, inside])
            mixed_yz = dy_ref[z + 2, rows] - dy_ref[z, rows]
            rhs_ref[z, rows] = exc_ref[z, rows] + (
                coef_ref[0, b : b + 1] * mixed_xy
                + coef_ref[1, b : b + 1] * mixed_xz
                + coef_ref[2, b : b + 1] * mixed_yz
            )
    ihigh_ref[...], ilow_ref[...] = split(inv_ref[...])


def stencil(table, potential, excited, inner, outer, region, inverse_x):
    nz, ny, nx = potential.shape
    half = pltpu.VMEM((nx, nx), jnp.bfloat16)
    return pl.pallas_call(
        stencil_kernel,
        in_specs=[SMEM] + [VMEM] * 6,
        out_specs=[VMEM] * 4,
        out_shape=[
            pltpu.VMEM((nz, ny, nx), jnp.float32),
            pltpu.VMEM((3, ny // 8, nx), jnp.float32),
            half,
            half,
        ],
        scratch_shapes=[
            pltpu.VMEM((nz + 2, ny + 16, nx), jnp.float32),
            pltpu.VMEM((nz + 2, ny, nx), jnp.float32),
        ],
        compiler_params=pltpu.CompilerParams(vmem_limit_bytes=32 * 1024 * 1024),
        cost_estimate=pl.CostEstimate(
            flops=60 * nz * ny * nx, bytes_accessed=20 * nz * ny * nx, transcendentals=0
        ),
        name="stencil",
    )(table, potential, excited, inner, outer, region, inverse_x)


def line_kernel(
    rhs_ref, inner_ref, outer_ref, coef_ref, ihigh_ref, ilow_ref,
    out_ref, edge_ref, high_ref, low_ref,
):
    nz, ny, nx = rhs_ref.shape
    half = nx // 2
    matrix = ihigh_ref[...], ilow_ref[...]
    sides = ordered(lax.axis_index("gy") % 2, inner_ref[...], outer_ref[...])
    for side, block, sign in ((0, 0, -1.0), (1, ny // 8 - 1, 1.0)):
        line = sides[side]
        row = slice(block, block + 1)
        mixed = coef_ref[0, row] * lane_difference(line)[1 : nz + 1] + coef_ref[2, row] * (
            line[2 : nz + 2] - line[:nz]
        )
        edge_ref[side] = sign * mixed
    row = lax.broadcasted_iota(jnp.int32, (8, nx), 0)
    first = lax.broadcasted_iota(jnp.int32, (half, 2 * ny), 1) < ny
    for z in range(nz):
        for b in range(ny // 8):
            part = rhs_ref[z, 8 * b : 8 * b + 8]
            if b == 0:
                part = part + jnp.where(row == 0, edge_ref[0, z : z + 1], 0.0)
            if b == ny // 8 - 1:
                part = part + jnp.where(row == 7, edge_ref[1, z : z + 1], 0.0)
            rows = slice(z * ny + 8 * b, z * ny + 8 * b + 8)
            high_ref[rows], low_ref[rows] = split(part)
    for z in range(0, nz, 2):
        rows = slice(z * ny, (z + 2) * ny)
        solved = product(matrix, (high_ref[rows], low_ref[rows]), NT)
        lower, upper = solved[:half], solved[half:]
        out_ref[:, z, :] = jnp.where(first, lower, pltpu.roll(upper, ny, 1))
        out_ref[:, z + 1, :] = jnp.where(first, pltpu.roll(lower, ny, 1), upper)


def line_solve(rhs, inner, outer, coefs, inv_high, inv_low):
    nz, ny, nx = rhs.shape
    return pl.pallas_call(
        line_kernel,
        in_specs=[VMEM] * 6,
        out_specs=VMEM,
        out_shape=jax.ShapeDtypeStruct((nx // 2, nz, 2 * ny), jnp.float32),
        scratch_shapes=[
            pltpu.VMEM((2, nz, nx), jnp.float32),
            pltpu.VMEM((nz * ny, nx), jnp.bfloat16),
            pltpu.VMEM((nz * ny, nx), jnp.bfloat16),
        ],
        compiler_params=pltpu.CompilerParams(vmem_limit_bytes=32 * 1024 * 1024),
        cost_estimate=pl.CostEstimate(
            flops=6 * nz * ny * nx * nx, bytes_accessed=12 * nz * ny * nx, transcendentals=0
        ),
        name="line_solve",
    )(rhs, inner, outer, coefs, inv_high, inv_low)


def plane_kernel(in_ref, invz_ref, invy_ref, out_ref, high_ref, low_ref):
    slabs, blocks, depth, width = in_ref.shape
    half = width // 2
    rows = slabs * depth
    matz, maty = split(invz_ref[...]), split(invy_ref[...])
    first = lax.broadcasted_iota(jnp.int32, (rows, width), 1) < half
    for b in range(0, blocks, 2):
        pair = []
        for k in (b, b + 1):
            pair.append(in_ref[:, k].reshape(rows, width))
        solved = product(matz, split(jnp.concatenate(pair, axis=1)), NN)
        left, right = solved[:, :width], solved[:, width:]
        columns = slice(b * half, (b + 2) * half)
        high_ref[:rows, columns], low_ref[:rows, columns] = split(
            jnp.where(first, left, pltpu.roll(right, half, 1))
        )
        high_ref[rows:, columns], low_ref[rows:, columns] = split(
            jnp.where(first, pltpu.roll(left, half, 1), right)
        )
    for b in range(0, blocks, 2):
        columns = slice(b * half, (b + 2) * half)
        solved = product(
            (high_ref[...], low_ref[...]), (maty[0][columns], maty[1][columns]), NT
        )
        one, two = solved[:rows], solved[rows:]
        out_ref[:, b] = jnp.where(first, one, pltpu.roll(two, half, 1)).reshape(slabs, depth, width)
        out_ref[:, b + 1] = jnp.where(first, pltpu.roll(one, half, 1), two).reshape(
            slabs, depth, width
        )


def plane_solve(planes, inverse_z, inverse_y):
    slabs, blocks, depth, width = planes.shape
    nz, ny = inverse_z.shape[0], inverse_y.shape[0]
    return pl.pallas_call(
        plane_kernel,
        in_specs=[VMEM] * 3,
        out_specs=VMEM,
        out_shape=jax.ShapeDtypeStruct(planes.shape, jnp.float32),
        scratch_shapes=[pltpu.VMEM((2 * nz, ny), jnp.bfloat16)] * 2,
        compiler_params=pltpu.CompilerParams(vmem_limit_bytes=40 * 1024 * 1024),
        cost_estimate=pl.CostEstimate(
            flops=12 * nz * ny * (nz + ny), bytes_accessed=16 * nz * ny, transcendentals=0
        ),
        name="plane_solve",
    )(planes, inverse_z, inverse_y)


def unpack_kernel(in_ref, out_ref):
    sources, depth, width = in_ref.shape
    ny = width // 2
    for z in range(depth):
        turned = in_ref[:, z, :].T
        out_ref[z, :, :sources] = turned[:ny]
        out_ref[z, :, sources:] = turned[ny:]


def unpack(tiles):
    sources, depth, width = tiles.shape
    return pl.pallas_call(
        unpack_kernel,
        in_specs=[VMEM],
        out_specs=VMEM,
        out_shape=jax.ShapeDtypeStruct((depth, width // 2, 2 * sources), jnp.float32),
        cost_estimate=pl.CostEstimate(
            flops=0, bytes_accessed=8 * sources * depth * width, transcendentals=0
        ),
        name="unpack",
    )(tiles)


def swaps(axis, inner, outer):
    count = lax.axis_size(axis)

    def both(first):
        pairs = [(i, i + 1) for i in range(first, count - 1, 2)]
        return pairs + [(j, i) for i, j in pairs]

    return lax.ppermute(outer, axis, both(1)), lax.ppermute(inner, axis, both(0))


def shards(
    potential,
    fast_gate,
    slow_gate,
    tissue,
    region_ids,
    fibre_table,
    inverse_x,
    inverse_z,
    inverse_y,
):
    odd = lax.axis_index("gz") % 2
    first, last = potential[0], potential[-1]
    z_outer, z_inner = swaps(
        "gz", jnp.where(odd == 1, first, last), jnp.where(odd == 1, last, first)
    )
    held, excited, row_low, row_high, new_fast, new_slow = ionic(
        potential, fast_gate, slow_gate, tissue
    )
    z_outer, z_inner, row_low, row_high = lax.optimization_barrier(
        (z_outer, z_inner, row_low, row_high)
    )
    last = z_inner.shape[0] - 1
    below, above = ordered(odd, z_inner[::last], z_outer[::last])
    row_low = jnp.concatenate([below[:1], row_low, above[:1]], axis=0)
    row_high = jnp.concatenate([below[1:], row_high, above[1:]], axis=0)
    odd = lax.axis_index("gy") % 2
    y_outer, y_inner = swaps(
        "gy", jnp.where(odd == 1, row_low, row_high), jnp.where(odd == 1, row_high, row_low)
    )
    rhs, coefs, inv_high, inv_low = stencil(
        fibre_table, held, excited, z_inner, z_outer, region_ids[0], inverse_x
    )
    tiles = line_solve(rhs, y_inner, y_outer, coefs, inv_high, inv_low)
    axes = ("gz", "gy")
    planes = lax.all_to_all(tiles, axes, split_axis=0, concat_axis=0, tiled=True)
    slabs, blocks = lax.axis_size("gz"), lax.axis_size("gy")
    solved = plane_solve(planes.reshape((slabs, blocks) + planes.shape[1:]), inverse_z, inverse_y)
    back = lax.all_to_all(
        solved.reshape(planes.shape), axes, split_axis=0, concat_axis=0, tiled=True
    )
    return (unpack(back), new_fast, new_slow)


def solution(mesh):
    return jax.shard_map(
        shards,
        mesh=mesh,
        in_specs=(
            P("gz", "gy", None),
            P("gz", "gy", None),
            P("gz", "gy", None),
            P("gz", "gy", None),
            P("gz", "gy", None),
            P(),
            P(),
            P(),
            P(),
        ),
        out_specs=(P("gz", "gy", None), P("gz", "gy", None), P("gz", "gy", None)),
        check_vma=False,
    )
```

```python
import math

import jax
import jax.numpy as jnp
from jax import lax
from jax.experimental import pallas as pl
from jax.experimental.pallas import tpu as pltpu
from jax.sharding import PartitionSpec as P

time_step = 0.1
depol_tau = 0.25
repol_tau = 33.33
inward_tau = 29.0
outward_tau = 12.5
vclose_tau = 3.33
vopen_high = 19.6
vopen_low = 1250.0
wclose_tau = 870.0
wopen_tau = 41.0
gate_crit = 0.13
vgate_crit = 0.04
inward_crit = 0.85
inward_slope = 10.0

VMEM = pl.BlockSpec(memory_space=pltpu.VMEM)
HBM = pl.BlockSpec(memory_space=pltpu.HBM)
NT = (((1,), (1,)), ((), ()))
NN = (((1,), (0,)), ((), ()))


def decay(tau):
    return math.exp(-time_step / tau)


def split(values):
    high = values.astype(jnp.bfloat16)
    return high, (values - high.astype(jnp.float32)).astype(jnp.bfloat16)


def product(left, right, dims):
    (lh, ll), (rh, rl) = left, right

    def dot(a, b):
        return lax.dot_general(a, b, dims, preferred_element_type=jnp.float32)

    return dot(lh, rh) + (dot(lh, rl) + dot(ll, rh))


def pinned(*arrays):
    return [pltpu.with_memory_space_constraint(array, pltpu.HBM) for array in arrays]


def faces_kernel(pot_ref, inner_ref, outer_ref, sems):
    odd = lax.axis_index("gz") % 2
    last = pot_ref.shape[0] - 1
    copies = [
        pltpu.make_async_copy(pot_ref.at[last * (1 - odd)], inner_ref, sems.at[0]),
        pltpu.make_async_copy(pot_ref.at[last * odd], outer_ref, sems.at[1]),
    ]
    for copy in copies:
        copy.start()
    for copy in copies:
        copy.wait()


def faces(potential):
    plane = pltpu.VMEM(potential.shape[1:], jnp.float32)
    return pl.pallas_call(
        faces_kernel,
        in_specs=[HBM],
        out_specs=[VMEM] * 2,
        out_shape=[plane] * 2,
        scratch_shapes=[pltpu.SemaphoreType.DMA((2,))],
        name="faces",
    )(*pinned(potential))


def ionic_kernel(
    table_ref, pot_ref, fast_ref, slow_ref, tissue_ref, region_ref, inv_ref,
    potc_ref, exc_ref, rows_ref, coef_ref, ihigh_ref, ilow_ref, nfast_ref, nslow_ref,
    fast_v, slow_v, tissue_v, region_v, inv_v, nfast_v, nslow_v, table_s,
    in_sems, out_sems, sems,
):
    nz, ny, nx = pot_ref.shape
    extra = [
        pltpu.make_async_copy(region_ref, region_v, sems.at[0]),
        pltpu.make_async_copy(inv_ref, inv_v, sems.at[1]),
        pltpu.make_async_copy(table_ref, table_s, sems.at[2]),
    ]
    pairs = ((pot_ref, potc_ref), (fast_ref, fast_v), (slow_ref, slow_v), (tissue_ref, tissue_v))
    loads = [
        [
            pltpu.make_async_copy(source.at[z], target.at[z], in_sems.at[k, z])
            for k, (source, target) in enumerate(pairs)
        ]
        for z in range(nz)
    ]
    stores = [
        [
            pltpu.make_async_copy(source.at[z], target.at[z], out_sems.at[k, z])
            for k, (source, target) in enumerate(((nfast_v, nfast_ref), (nslow_v, nslow_ref)))
        ]
        for z in range(nz)
    ]
    for group in loads:
        for copy in group:
            copy.start()
    for copy in extra:
        copy.start()
    for z in range(nz):
        for copy in loads[z]:
            copy.wait()
        for row in range(0, ny, 8):
            rows = (z, slice(row, row + 8))
            p, v, w = potc_ref[rows], fast_v[rows], slow_v[rows]
            living = tissue_v[rows] == 1
            active = p >= gate_crit
            exc_ref[rows] = jnp.where(living, excite(p, v, w, active), p)
            target = jnp.where(active, 0.0, 1.0)
            keep_fast = jnp.where(
                active,
                decay(vclose_tau),
                jnp.where(p >= vgate_crit, decay(vopen_high), decay(vopen_low)),
            )
            keep_slow = jnp.where(active, decay(wclose_tau), decay(wopen_tau))
            nfast_v[rows] = jnp.where(living, target + (v - target) * keep_fast, v)
            nslow_v[rows] = jnp.where(living, target + (w - target) * keep_slow, w)
        for copy in stores[z]:
            copy.start()
        for k, line in enumerate((potc_ref[z, 0:1], potc_ref[z, 1:2], exc_ref[z, 0:1])):
            rows_ref[k * nz + z : k * nz + z + 1] = line
    for copy in extra:
        copy.wait()
    for column, coef in enumerate(coefficients(table_s, region_v, nx)):
        coef_ref[column] = coef
    ihigh_ref[...], ilow_ref[...] = split(inv_v[...])
    for group in stores:
        for copy in group:
            copy.wait()


def ionic(table, potential, fast_gate, slow_gate, tissue, region, inverse_x):
    nz, ny, nx = potential.shape
    shape = jax.ShapeDtypeStruct((nz, ny, nx), jnp.float32)
    field = pltpu.VMEM((nz, ny, nx), jnp.float32)
    part = pltpu.VMEM((nx, nx), jnp.bfloat16)
    return pl.pallas_call(
        ionic_kernel,
        in_specs=[HBM] * 7,
        out_specs=[VMEM] * 6 + [HBM] * 2,
        out_shape=[
            field,
            field,
            pltpu.VMEM((3 * nz, nx), jnp.float32),
            pltpu.VMEM((3, ny // 8, nx), jnp.float32),
            part,
            part,
            shape,
            shape,
        ],
        scratch_shapes=[
            field,
            field,
            pltpu.VMEM((nz, ny, nx), jnp.int32),
            pltpu.VMEM(region.shape, jnp.int32),
            pltpu.VMEM((nx, nx), jnp.float32),
            field,
            field,
            pltpu.SMEM(table.shape, jnp.float32),
            pltpu.SemaphoreType.DMA((4, nz)),
            pltpu.SemaphoreType.DMA((2, nz)),
            pltpu.SemaphoreType.DMA((3,)),
        ],
        compiler_params=pltpu.CompilerParams(vmem_limit_bytes=16 * 1024 * 1024),
        cost_estimate=pl.CostEstimate(
            flops=40 * nz * ny * nx, bytes_accessed=28 * nz * ny * nx, transcendentals=0
        ),
        name="ionic",
    )(*pinned(table, potential, fast_gate, slow_gate, tissue, region, inverse_x))


def excite(p, v, w, active):
    current = jnp.where(
        active,
        (1.0 / repol_tau) - v * (1.0 - p) * (p - gate_crit) * (1.0 / depol_tau),
        p * (1.0 / outward_tau),
    )
    current = current - w * (1.0 + jnp.tanh(inward_slope * (p - inward_crit))) * (
        1.0 / (2.0 * inward_tau)
    )
    return p - time_step * current


def lane_difference(values):
    width = values.shape[-1]
    lane = lax.broadcasted_iota(jnp.int32, values.shape, values.ndim - 1)
    ahead = pltpu.roll(values, width - 1, values.ndim - 1)
    behind = pltpu.roll(values, 1, values.ndim - 1)
    return jnp.where(lane == width - 1, 0.0, ahead) - jnp.where(lane == 0, 0.0, behind)


def coefficients(table_ref, region_ref, nx):
    blocks = region_ref.shape[1]
    spread = (
        lax.broadcasted_iota(jnp.int32, (blocks, nx), 1) // 8
        == lax.broadcasted_iota(jnp.int32, (blocks, nx), 0)
    ).astype(jnp.bfloat16)
    ids = lax.dot_general(
        region_ref[...].astype(jnp.float32).astype(jnp.bfloat16), spread, NN,
        preferred_element_type=jnp.float32,
    )
    coefs = []
    for column in range(3):
        coef = jnp.zeros_like(ids)
        for region in range(table_ref.shape[1]):
            coef = jnp.where(ids == float(region), 0.5 * table_ref[column, region], coef)
        coefs.append(coef)
    return coefs


def ordered(odd, inner, outer):
    return jnp.where(odd == 1, inner, outer), jnp.where(odd == 1, outer, inner)


def message_kernel(rows_ref, coef_ref, inner_ref, outer_ref, out_ref, pad_ref):
    nz = rows_ref.shape[0] // 3
    pads = nz + 2
    odd = lax.axis_index("gz") % 2
    for k in range(2):
        row = slice(k, k + 1)
        below, above = ordered(odd, inner_ref[row], outer_ref[row])
        pad_ref[k, 0:1] = below
        pad_ref[k, 1 : nz + 1] = rows_ref[k * nz : (k + 1) * nz]
        pad_ref[k, nz + 1 : pads] = above
    out_ref[0:nz] = rows_ref[2 * nz :] + (
        coef_ref[0, 0:1] * lane_difference(pad_ref[1, 1 : nz + 1])
        + coef_ref[1, 0:1] * lane_difference(pad_ref[0, 2:pads] - pad_ref[0, 0:nz])
        + coef_ref[2, 0:1] * (pad_ref[1, 2:pads] - pad_ref[1, 0:nz])
    )
    out_ref[nz : nz + pads] = pad_ref[0, 0:pads]
    out_ref[nz + pads : nz + pads + 1] = coef_ref[0, 0:1]
    out_ref[nz + pads + 1 : nz + pads + 2] = coef_ref[2, 0:1]
    rest = out_ref.shape[0] - (nz + pads + 2)
    out_ref[nz + pads + 2 :] = jnp.zeros((rest, out_ref.shape[1]), jnp.float32)


def message(rows, coefs, inner, outer):
    nz, nx = rows.shape[0] // 3, rows.shape[1]
    return pl.pallas_call(
        message_kernel,
        in_specs=[VMEM] * 4,
        out_specs=VMEM,
        out_shape=pltpu.VMEM((3 * nz, nx), jnp.float32),
        scratch_shapes=[pltpu.VMEM((2, 16, nx), jnp.float32)],
        compiler_params=pltpu.CompilerParams(vmem_limit_bytes=4 * 1024 * 1024),
        name="message",
    )(rows, coefs, inner, outer)


def stencil_kernel(
    pot_ref, exc_ref, coef_ref, inner_ref, outer_ref, ihigh_ref, ilow_ref, invz_ref, invy_ref,
    out_ref, line_ref, zhigh_ref, zlow_ref, yhigh_ref, ylow_ref,
    pad_ref, dy_ref, high_ref, low_ref, invz_v, invy_v, sems,
):
    nz, ny, nx = pot_ref.shape
    half = nx // 2
    loads = [
        pltpu.make_async_copy(invz_ref, invz_v, sems.at[0]),
        pltpu.make_async_copy(invy_ref, invy_v, sems.at[1]),
    ]
    for copy in loads:
        copy.start()
    below, above = ordered(lax.axis_index("gz") % 2, inner_ref[...], outer_ref[...])
    nothing = jnp.zeros((1, nx), jnp.float32)
    for z in range(nz + 2):
        plane = below if z == 0 else above if z == nz + 1 else pot_ref[z - 1]
        pad_ref[z, 8 : 8 + ny] = plane
        pad_ref[z, 7:8] = nothing
        pad_ref[z, 8 + ny : 9 + ny] = nothing
        dy_ref[z] = pad_ref[z, 9 : 9 + ny] - pad_ref[z, 7 : 7 + ny]
        line_ref[z : z + 1] = plane[ny - 1 :]
    row = lax.broadcasted_iota(jnp.int32, (8, nx), 0)
    first = lax.broadcasted_iota(jnp.int32, (half, 2 * ny), 1) < ny
    matrix = ihigh_ref[...], ilow_ref[...]
    blocks = ny // 8
    for z in range(nz):
        parts = []
        for b in range(blocks):
            rows = slice(8 * b, 8 * b + 8)
            inside = slice(8 * b + 8, 8 * b + 16)
            mixed_xy = lane_difference(dy_ref[z + 1, rows])
            mixed_xz = lane_difference(pad_ref[z + 2, inside] - pad_ref[z, inside])
            mixed_yz = dy_ref[z + 2, rows] - dy_ref[z, rows]
            parts.append(
                exc_ref[z, rows]
                + (
                    coef_ref[0, b : b + 1] * mixed_xy
                    + coef_ref[1, b : b + 1] * mixed_xz
                    + coef_ref[2, b : b + 1] * mixed_yz
                )
            )
        middle, last = parts[blocks // 2], parts[-1]
        parts[0] = jnp.where(row == 0, 0.0, parts[0])
        parts[blocks // 2] = jnp.where(row == 0, last[7:8], middle)
        parts[-1] = jnp.where(row == 7, middle[0:1], last)
        for b in range(0, blocks, 2):
            rows = slice(z * ny + 8 * b, z * ny + 8 * b + 16)
            high_ref[rows], low_ref[rows] = split(jnp.concatenate(parts[b : b + 2], axis=0))
        if z % 2 == 1:
            rows = slice((z - 1) * ny, (z + 1) * ny)
            solved = product(matrix, (high_ref[rows], low_ref[rows]), NT)
            lower, upper = solved[:half], solved[half:]
            out_ref[:, z - 1, :] = jnp.where(first, lower, pltpu.roll(upper, ny, 1))
            out_ref[:, z, :] = jnp.where(first, pltpu.roll(lower, ny, 1), upper)
    for copy in loads:
        copy.wait()
    zhigh_ref[...], zlow_ref[...] = split(invz_v[...])
    width = invy_v.shape[1]
    invy = invy_v[...]
    slot = lax.broadcasted_iota(jnp.int32, invy.shape, 1) % ny
    move = ny // 2 - 1
    yhigh_ref[...], ylow_ref[...] = split(
        jnp.where(
            slot == 0,
            pltpu.roll(invy, width - ny, 1),
            jnp.where(
                slot == ny // 2,
                pltpu.roll(invy, width - move, 1),
                jnp.where(slot == ny - 1, pltpu.roll(invy, move, 1), invy),
            ),
        )
    )


def stencil(potential, excited, coefs, inner, outer, inv_high, inv_low, inverse_z, inverse_y):
    nz, ny, nx = potential.shape
    return pl.pallas_call(
        stencil_kernel,
        in_specs=[VMEM] * 7 + [HBM] * 2,
        out_specs=[VMEM] * 6,
        out_shape=[
            pltpu.VMEM((nx // 2, nz, 2 * ny), jnp.float32),
            pltpu.VMEM((nz + 2, nx), jnp.float32),
        ]
        + [pltpu.VMEM(inverse_z.shape, jnp.bfloat16)] * 2
        + [pltpu.VMEM(inverse_y.shape, jnp.bfloat16)] * 2,
        scratch_shapes=[
            pltpu.VMEM((nz + 2, ny + 16, nx), jnp.float32),
            pltpu.VMEM((nz + 2, ny, nx), jnp.float32),
            pltpu.VMEM((nz * ny, nx), jnp.bfloat16),
            pltpu.VMEM((nz * ny, nx), jnp.bfloat16),
            pltpu.VMEM(inverse_z.shape, jnp.float32),
            pltpu.VMEM(inverse_y.shape, jnp.float32),
            pltpu.SemaphoreType.DMA((2,)),
        ],
        compiler_params=pltpu.CompilerParams(vmem_limit_bytes=20 * 1024 * 1024),
        cost_estimate=pl.CostEstimate(
            flops=6 * nz * ny * nx * nx, bytes_accessed=24 * nz * ny * nx, transcendentals=0
        ),
        name="stencil",
    )(potential, excited, coefs, inner, outer, inv_high, inv_low, *pinned(inverse_z, inverse_y))


def patch_kernel(
    in_ref, line_ref, coef_ref, sent_ref, ihigh_ref, ilow_ref, out_ref, rhs_ref, dy_ref
):
    half, nz, width = in_ref.shape
    ny = width // 2
    pads = nz + 2
    keep = jnp.where(lax.axis_index("gy") == lax.axis_size("gy") - 1, 0.0, 1.0)
    inside = slice(1, nz + 1)
    row = slice(coef_ref.shape[1] - 1, coef_ref.shape[1])
    dy_ref[0:pads] = sent_ref[nz : nz + pads] * keep
    last = coef_ref[0, row] * lane_difference(dy_ref[inside]) + coef_ref[2, row] * (
        dy_ref[2:pads] - dy_ref[0:nz]
    )
    dy_ref[0:pads] = line_ref[...] * keep
    end = nz + pads
    extra = sent_ref[0:nz] - (
        sent_ref[end : end + 1] * lane_difference(dy_ref[inside])
        + sent_ref[end + 1 : end + 2] * (dy_ref[2:pads] - dy_ref[0:nz])
    )
    rhs_ref[...] = jnp.zeros_like(rhs_ref)
    rhs_ref[0:nz] = extra
    rhs_ref[ny // 2 : ny // 2 + nz] = last
    solved = product((ihigh_ref[...], ilow_ref[...]), split(rhs_ref[...]), NT)
    lane = lax.broadcasted_iota(jnp.int32, (half, width), 1)
    both = jnp.where(lane < ny, solved[:half], pltpu.roll(solved[half:], ny, 1))
    for z in range(nz):
        moved = pltpu.roll(both, width - z, 1) if z else both
        out_ref[:, z, :] = in_ref[:, z, :] + jnp.where(lane % (ny // 2) == 0, moved, 0.0)


def patch(tiles, line, coefs, sent, inv_high, inv_low):
    half, nz, width = tiles.shape
    nx = 2 * half
    return pl.pallas_call(
        patch_kernel,
        in_specs=[VMEM] * 6,
        out_specs=VMEM,
        out_shape=pltpu.VMEM(tiles.shape, jnp.float32),
        scratch_shapes=[
            pltpu.VMEM((width, nx), jnp.float32),
            pltpu.VMEM((16, nx), jnp.float32),
        ],
        compiler_params=pltpu.CompilerParams(vmem_limit_bytes=16 * 1024 * 1024),
        cost_estimate=pl.CostEstimate(
            flops=6 * width * nx * nx, bytes_accessed=8 * half * nz * width, transcendentals=0
        ),
        name="patch",
    )(tiles, line, coefs, sent, inv_high, inv_low)


def plane_kernel(
    in_ref, zhigh_ref, zlow_ref, yhigh_ref, ylow_ref, out_ref, high_ref, low_ref
):
    slabs, blocks, depth, width = in_ref.shape
    half = width // 2
    rows = slabs * depth
    matz = zhigh_ref[...], zlow_ref[...]
    first = lax.broadcasted_iota(jnp.int32, (rows, width), 1) < half
    for b in range(0, blocks, 2):
        pair = []
        for k in (b, b + 1):
            pair.append(in_ref[:, k].reshape(rows, width))
        solved = product(matz, split(jnp.concatenate(pair, axis=1)), NN)
        left, right = solved[:, :width], solved[:, width:]
        columns = slice(b * half, (b + 2) * half)
        high_ref[:rows, columns], low_ref[:rows, columns] = split(
            jnp.where(first, left, pltpu.roll(right, half, 1))
        )
        high_ref[rows:, columns], low_ref[rows:, columns] = split(
            jnp.where(first, pltpu.roll(left, half, 1), right)
        )
    for b in range(0, blocks, 2):
        columns = slice(b * half, (b + 2) * half)
        solved = product(
            (high_ref[...], low_ref[...]), (yhigh_ref[columns], ylow_ref[columns]), NT
        )
        one, two = solved[:rows], solved[rows:]
        out_ref[:, b] = jnp.where(first, one, pltpu.roll(two, half, 1)).reshape(slabs, depth, width)
        out_ref[:, b + 1] = jnp.where(first, pltpu.roll(one, half, 1), two).reshape(
            slabs, depth, width
        )


def plane_solve(planes, *matrices):
    slabs, blocks, depth, width = planes.shape
    nz, ny = matrices[0].shape[0], matrices[-1].shape[0]
    return pl.pallas_call(
        plane_kernel,
        in_specs=[VMEM] * 5,
        out_specs=VMEM,
        out_shape=jax.ShapeDtypeStruct(planes.shape, jnp.float32),
        scratch_shapes=[pltpu.VMEM((2 * nz, ny), jnp.bfloat16)] * 2,
        compiler_params=pltpu.CompilerParams(vmem_limit_bytes=16 * 1024 * 1024),
        cost_estimate=pl.CostEstimate(
            flops=12 * nz * ny * (nz + ny), bytes_accessed=16 * nz * ny, transcendentals=0
        ),
        name="plane_solve",
    )(planes, *matrices)


def unpack_kernel(in_ref, out_ref, turned_ref, sems):
    sources, depth, width = in_ref.shape
    ny = width // 2
    copies = []
    for z in range(depth):
        turned = in_ref[:, z, :].T
        turned_ref[z, :, :sources] = turned[:ny]
        turned_ref[z, :, sources:] = turned[ny:]
        copies.append(pltpu.make_async_copy(turned_ref.at[z], out_ref.at[z], sems.at[z]))
        copies[-1].start()
    for copy in copies:
        copy.wait()


def unpack(tiles):
    sources, depth, width = tiles.shape
    shape = (depth, width // 2, 2 * sources)
    return pl.pallas_call(
        unpack_kernel,
        in_specs=[VMEM],
        out_specs=HBM,
        out_shape=jax.ShapeDtypeStruct(shape, jnp.float32),
        scratch_shapes=[pltpu.VMEM(shape, jnp.float32), pltpu.SemaphoreType.DMA((depth,))],
        cost_estimate=pl.CostEstimate(
            flops=0, bytes_accessed=8 * sources * depth * width, transcendentals=0
        ),
        name="unpack",
    )(pltpu.with_memory_space_constraint(tiles, pltpu.VMEM))


def swaps(axis, inner, outer):
    count = lax.axis_size(axis)

    def both(first):
        pairs = [(i, i + 1) for i in range(first, count - 1, 2)]
        return pairs + [(j, i) for i, j in pairs]

    return lax.ppermute(outer, axis, both(1)), lax.ppermute(inner, axis, both(0))


def shards(
    potential,
    fast_gate,
    slow_gate,
    tissue,
    region_ids,
    fibre_table,
    inverse_x,
    inverse_z,
    inverse_y,
):
    inner, outer = faces(potential)
    z_outer, z_inner = swaps("gz", inner, outer)
    held, excited, rows, coefs, inv_high, inv_low, new_fast, new_slow = ionic(
        fibre_table.T, potential, fast_gate, slow_gate, tissue, region_ids[0], inverse_x
    )
    z_outer, z_inner, rows, coefs = lax.optimization_barrier((z_outer, z_inner, rows, coefs))
    count = lax.axis_size("gy")
    sent = lax.ppermute(
        message(rows, coefs, z_inner, z_outer), "gy", [((i + 1) % count, i) for i in range(count)]
    )
    tiles, line, *matrices = stencil(
        held, excited, coefs, z_inner, z_outer, inv_high, inv_low, inverse_z, inverse_y
    )
    tiles = patch(tiles, line, coefs, sent, inv_high, inv_low)
    axes = ("gz", "gy")
    planes = lax.all_to_all(tiles, axes, split_axis=0, concat_axis=0, tiled=True)
    slabs, blocks = lax.axis_size("gz"), lax.axis_size("gy")
    solved = plane_solve(planes.reshape((slabs, blocks) + planes.shape[1:]), *matrices)
    back = lax.all_to_all(
        solved.reshape(planes.shape), axes, split_axis=0, concat_axis=0, tiled=True
    )
    return (unpack(back), new_fast, new_slow)


def solution(mesh):
    return jax.shard_map(
        shards,
        mesh=mesh,
        in_specs=(
            P("gz", "gy", None),
            P("gz", "gy", None),
            P("gz", "gy", None),
            P("gz", "gy", None),
            P("gz", "gy", None),
            P(),
            P(),
            P(),
            P(),
        ),
        out_specs=(P("gz", "gy", None), P("gz", "gy", None), P("gz", "gy", None)),
        check_vma=False,
    )
```

```python
import math

import jax
import jax.numpy as jnp
from jax import lax
from jax.experimental import pallas as pl
from jax.experimental.pallas import tpu as pltpu
from jax.sharding import PartitionSpec as P

time_step = 0.1
depol_tau = 0.25
repol_tau = 33.33
inward_tau = 29.0
outward_tau = 12.5
vclose_tau = 3.33
vopen_high = 19.6
vopen_low = 1250.0
wclose_tau = 870.0
wopen_tau = 41.0
gate_crit = 0.13
vgate_crit = 0.04
inward_crit = 0.85
inward_slope = 10.0

VMEM = pl.BlockSpec(memory_space=pltpu.VMEM)
HBM = pl.BlockSpec(memory_space=pltpu.HBM)
NT = (((1,), (1,)), ((), ()))
NN = (((1,), (0,)), ((), ()))


def decay(tau):
    return math.exp(-time_step / tau)


def split(values):
    high = values.astype(jnp.bfloat16)
    return high, (values - high.astype(jnp.float32)).astype(jnp.bfloat16)


def product(left, right, dims):
    (lh, ll), (rh, rl) = left, right

    def dot(a, b):
        return lax.dot_general(a, b, dims, preferred_element_type=jnp.float32)

    return dot(lh, rh) + (dot(lh, rl) + dot(ll, rh))


def pinned(*arrays):
    return [pltpu.with_memory_space_constraint(array, pltpu.HBM) for array in arrays]


def faces_kernel(pot_ref, inner_ref, outer_ref, sems):
    odd = lax.axis_index("gz") % 2
    last = pot_ref.shape[0] - 1
    copies = [
        pltpu.make_async_copy(pot_ref.at[last * (1 - odd)], inner_ref, sems.at[0]),
        pltpu.make_async_copy(pot_ref.at[last * odd], outer_ref, sems.at[1]),
    ]
    for copy in copies:
        copy.start()
    for copy in copies:
        copy.wait()


def faces(potential):
    plane = pltpu.VMEM(potential.shape[1:], jnp.float32)
    return pl.pallas_call(
        faces_kernel,
        in_specs=[HBM],
        out_specs=[VMEM] * 2,
        out_shape=[plane] * 2,
        scratch_shapes=[pltpu.SemaphoreType.DMA((2,))],
        name="faces",
    )(*pinned(potential))


def ionic_kernel(
    table_ref, pot_ref, fast_ref, slow_ref, tissue_ref, region_ref, inv_ref,
    potc_ref, exc_ref, rows_ref, coef_ref, ihigh_ref, ilow_ref, nfast_ref, nslow_ref,
    fast_v, slow_v, tissue_v, region_v, inv_v, table_s, in_sems, sems,
):
    nz, ny, nx = pot_ref.shape
    extra = [
        pltpu.make_async_copy(region_ref, region_v, sems.at[0]),
        pltpu.make_async_copy(inv_ref, inv_v, sems.at[1]),
        pltpu.make_async_copy(table_ref, table_s, sems.at[2]),
    ]
    pairs = ((pot_ref, potc_ref), (fast_ref, fast_v), (slow_ref, slow_v), (tissue_ref, tissue_v))
    loads = [
        [
            pltpu.make_async_copy(source.at[z], target.at[z], in_sems.at[k, z])
            for k, (source, target) in enumerate(pairs)
        ]
        for z in range(nz)
    ]
    for group in loads:
        for copy in group:
            copy.start()
    for copy in extra:
        copy.start()
    for z in range(nz):
        for copy in loads[z]:
            copy.wait()
        for row in range(0, ny, 8):
            rows = (z, slice(row, row + 8))
            p, v, w = potc_ref[rows], fast_v[rows], slow_v[rows]
            living = tissue_v[rows] == 1
            active = p >= gate_crit
            exc_ref[rows] = jnp.where(living, excite(p, v, w, active), p)
            target = jnp.where(active, 0.0, 1.0)
            keep_fast = jnp.where(
                active,
                decay(vclose_tau),
                jnp.where(p >= vgate_crit, decay(vopen_high), decay(vopen_low)),
            )
            keep_slow = jnp.where(active, decay(wclose_tau), decay(wopen_tau))
            nfast_ref[rows] = jnp.where(living, target + (v - target) * keep_fast, v)
            nslow_ref[rows] = jnp.where(living, target + (w - target) * keep_slow, w)
        for k, line in enumerate((potc_ref[z, 0:1], potc_ref[z, 1:2], exc_ref[z, 0:1])):
            rows_ref[k * nz + z : k * nz + z + 1] = line
    for copy in extra:
        copy.wait()
    for column, coef in enumerate(coefficients(table_s, region_v, nx)):
        coef_ref[column] = coef
    ihigh_ref[...], ilow_ref[...] = split(inv_v[...])


def ionic(table, potential, fast_gate, slow_gate, tissue, region, inverse_x):
    nz, ny, nx = potential.shape
    field = pltpu.VMEM((nz, ny, nx), jnp.float32)
    part = pltpu.VMEM((nx, nx), jnp.bfloat16)
    return pl.pallas_call(
        ionic_kernel,
        in_specs=[HBM] * 7,
        out_specs=[VMEM] * 8,
        out_shape=[
            field,
            field,
            pltpu.VMEM((3 * nz, nx), jnp.float32),
            pltpu.VMEM((3, ny // 8, nx), jnp.float32),
            part,
            part,
            field,
            field,
        ],
        scratch_shapes=[
            field,
            field,
            pltpu.VMEM((nz, ny, nx), jnp.int32),
            pltpu.VMEM(region.shape, jnp.int32),
            pltpu.VMEM((nx, nx), jnp.float32),
            pltpu.SMEM(table.shape, jnp.float32),
            pltpu.SemaphoreType.DMA((4, nz)),
            pltpu.SemaphoreType.DMA((3,)),
        ],
        compiler_params=pltpu.CompilerParams(vmem_limit_bytes=16 * 1024 * 1024),
        cost_estimate=pl.CostEstimate(
            flops=40 * nz * ny * nx, bytes_accessed=28 * nz * ny * nx, transcendentals=0
        ),
        name="ionic",
    )(*pinned(table, potential, fast_gate, slow_gate, tissue, region, inverse_x))


def excite(p, v, w, active):
    current = jnp.where(
        active,
        (1.0 / repol_tau) - v * (1.0 - p) * (p - gate_crit) * (1.0 / depol_tau),
        p * (1.0 / outward_tau),
    )
    current = current - w * (1.0 + jnp.tanh(inward_slope * (p - inward_crit))) * (
        1.0 / (2.0 * inward_tau)
    )
    return p - time_step * current


def lane_difference(values):
    width = values.shape[-1]
    lane = lax.broadcasted_iota(jnp.int32, values.shape, values.ndim - 1)
    ahead = pltpu.roll(values, width - 1, values.ndim - 1)
    behind = pltpu.roll(values, 1, values.ndim - 1)
    return jnp.where(lane == width - 1, 0.0, ahead) - jnp.where(lane == 0, 0.0, behind)


def coefficients(table_ref, region_ref, nx):
    blocks = region_ref.shape[1]
    spread = (
        lax.broadcasted_iota(jnp.int32, (blocks, nx), 1) // 8
        == lax.broadcasted_iota(jnp.int32, (blocks, nx), 0)
    ).astype(jnp.bfloat16)
    ids = lax.dot_general(
        region_ref[...].astype(jnp.float32).astype(jnp.bfloat16), spread, NN,
        preferred_element_type=jnp.float32,
    )
    coefs = []
    for column in range(3):
        coef = jnp.zeros_like(ids)
        for region in range(table_ref.shape[1]):
            coef = jnp.where(ids == float(region), 0.5 * table_ref[column, region], coef)
        coefs.append(coef)
    return coefs


def ordered(odd, inner, outer):
    return jnp.where(odd == 1, inner, outer), jnp.where(odd == 1, outer, inner)


def message_kernel(rows_ref, coef_ref, inner_ref, outer_ref, out_ref, pad_ref):
    nz = rows_ref.shape[0] // 3
    pads = nz + 2
    odd = lax.axis_index("gz") % 2
    for k in range(2):
        row = slice(k, k + 1)
        below, above = ordered(odd, inner_ref[row], outer_ref[row])
        pad_ref[k, 0:1] = below
        pad_ref[k, 1 : nz + 1] = rows_ref[k * nz : (k + 1) * nz]
        pad_ref[k, nz + 1 : pads] = above
    out_ref[0:nz] = rows_ref[2 * nz :] + (
        coef_ref[0, 0:1] * lane_difference(pad_ref[1, 1 : nz + 1])
        + coef_ref[1, 0:1] * lane_difference(pad_ref[0, 2:pads] - pad_ref[0, 0:nz])
        + coef_ref[2, 0:1] * (pad_ref[1, 2:pads] - pad_ref[1, 0:nz])
    )
    out_ref[nz : nz + pads] = pad_ref[0, 0:pads]
    out_ref[nz + pads : nz + pads + 1] = coef_ref[0, 0:1]
    out_ref[nz + pads + 1 : nz + pads + 2] = coef_ref[2, 0:1]
    rest = out_ref.shape[0] - (nz + pads + 2)
    out_ref[nz + pads + 2 :] = jnp.zeros((rest, out_ref.shape[1]), jnp.float32)


def message(rows, coefs, inner, outer):
    nz, nx = rows.shape[0] // 3, rows.shape[1]
    return pl.pallas_call(
        message_kernel,
        in_specs=[VMEM] * 4,
        out_specs=VMEM,
        out_shape=pltpu.VMEM((3 * nz, nx), jnp.float32),
        scratch_shapes=[pltpu.VMEM((2, 16, nx), jnp.float32)],
        compiler_params=pltpu.CompilerParams(vmem_limit_bytes=4 * 1024 * 1024),
        name="message",
    )(rows, coefs, inner, outer)


def stencil_kernel(
    pot_ref, exc_ref, coef_ref, inner_ref, outer_ref, ihigh_ref, ilow_ref, invz_ref, invy_ref,
    nfast_v, nslow_v,
    out_ref, line_ref, zhigh_ref, zlow_ref, yhigh_ref, ylow_ref, nfast_ref, nslow_ref,
    pad_ref, dy_ref, high_ref, low_ref, invz_v, invy_v, sems,
):
    nz, ny, nx = pot_ref.shape
    half = nx // 2
    loads = [
        pltpu.make_async_copy(invz_ref, invz_v, sems.at[0]),
        pltpu.make_async_copy(invy_ref, invy_v, sems.at[1]),
    ]
    stores = [
        pltpu.make_async_copy(nfast_v, nfast_ref, sems.at[2]),
        pltpu.make_async_copy(nslow_v, nslow_ref, sems.at[3]),
    ]
    for copy in loads + stores:
        copy.start()
    below, above = ordered(lax.axis_index("gz") % 2, inner_ref[...], outer_ref[...])
    nothing = jnp.zeros((1, nx), jnp.float32)
    for z in range(nz + 2):
        plane = below if z == 0 else above if z == nz + 1 else pot_ref[z - 1]
        pad_ref[z, 8 : 8 + ny] = plane
        pad_ref[z, 7:8] = nothing
        pad_ref[z, 8 + ny : 9 + ny] = nothing
        dy_ref[z] = pad_ref[z, 9 : 9 + ny] - pad_ref[z, 7 : 7 + ny]
        line_ref[z : z + 1] = plane[ny - 1 :]
    row = lax.broadcasted_iota(jnp.int32, (8, nx), 0)
    first = lax.broadcasted_iota(jnp.int32, (half, 2 * ny), 1) < ny
    matrix = ihigh_ref[...], ilow_ref[...]
    blocks = ny // 8
    for z in range(nz):
        parts = []
        for b in range(blocks):
            rows = slice(8 * b, 8 * b + 8)
            inside = slice(8 * b + 8, 8 * b + 16)
            mixed_xy = lane_difference(dy_ref[z + 1, rows])
            mixed_xz = lane_difference(pad_ref[z + 2, inside] - pad_ref[z, inside])
            mixed_yz = dy_ref[z + 2, rows] - dy_ref[z, rows]
            parts.append(
                exc_ref[z, rows]
                + (
                    coef_ref[0, b : b + 1] * mixed_xy
                    + coef_ref[1, b : b + 1] * mixed_xz
                    + coef_ref[2, b : b + 1] * mixed_yz
                )
            )
        parts[0] = jnp.where(row == 0, 0.0, parts[0])
        for b in range(0, blocks, 2):
            rows = slice(z * ny + 8 * b, z * ny + 8 * b + 16)
            high_ref[rows], low_ref[rows] = split(jnp.concatenate(parts[b : b + 2], axis=0))
        if z % 4 == 3:
            rows = slice((z - 3) * ny, (z + 1) * ny)
            solved = product(matrix, (high_ref[rows], low_ref[rows]), NT)
            for k in range(2):
                columns = slice(2 * k * ny, 2 * (k + 1) * ny)
                lower, upper = solved[:half, columns], solved[half:, columns]
                at = z - 3 + 2 * k
                out_ref[:, at, :] = jnp.where(first, lower, pltpu.roll(upper, ny, 1))
                out_ref[:, at + 1, :] = jnp.where(first, pltpu.roll(lower, ny, 1), upper)
    for copy in loads:
        copy.wait()
    zhigh_ref[...], zlow_ref[...] = split(invz_v[...])
    width = invy_v.shape[1]
    invy = invy_v[...]
    column = lax.broadcasted_iota(jnp.int32, invy.shape, 1)
    yhigh_ref[...], ylow_ref[...] = split(
        jnp.where(column % ny == 0, pltpu.roll(invy, width - ny, 1), invy)
    )
    for copy in stores:
        copy.wait()


def stencil(
    potential, excited, coefs, inner, outer, inv_high, inv_low, inverse_z, inverse_y, *gates
):
    nz, ny, nx = potential.shape
    return pl.pallas_call(
        stencil_kernel,
        in_specs=[VMEM] * 7 + [HBM] * 2 + [VMEM] * 2,
        out_specs=[VMEM] * 6 + [HBM] * 2,
        out_shape=[
            pltpu.VMEM((nx // 2, nz, 2 * ny), jnp.float32),
            pltpu.VMEM((nz + 2, nx), jnp.float32),
        ]
        + [pltpu.VMEM(inverse_z.shape, jnp.bfloat16)] * 2
        + [pltpu.VMEM(inverse_y.shape, jnp.bfloat16)] * 2
        + [jax.ShapeDtypeStruct((nz, ny, nx), jnp.float32)] * 2,
        scratch_shapes=[
            pltpu.VMEM((nz + 2, ny + 16, nx), jnp.float32),
            pltpu.VMEM((nz + 2, ny, nx), jnp.float32),
            pltpu.VMEM((nz * ny, nx), jnp.bfloat16),
            pltpu.VMEM((nz * ny, nx), jnp.bfloat16),
            pltpu.VMEM(inverse_z.shape, jnp.float32),
            pltpu.VMEM(inverse_y.shape, jnp.float32),
            pltpu.SemaphoreType.DMA((4,)),
        ],
        compiler_params=pltpu.CompilerParams(vmem_limit_bytes=24 * 1024 * 1024),
        cost_estimate=pl.CostEstimate(
            flops=6 * nz * ny * nx * nx, bytes_accessed=32 * nz * ny * nx, transcendentals=0
        ),
        name="stencil",
    )(
        potential, excited, coefs, inner, outer, inv_high, inv_low,
        *pinned(inverse_z, inverse_y), *gates,
    )


def patch_kernel(
    in_ref, line_ref, coef_ref, sent_ref, ihigh_ref, ilow_ref, out_ref, rhs_ref, dy_ref
):
    half, nz, width = in_ref.shape
    ny = width // 2
    pads = nz + 2
    keep = jnp.where(lax.axis_index("gy") == lax.axis_size("gy") - 1, 0.0, 1.0)
    inside = slice(1, nz + 1)
    row = slice(coef_ref.shape[1] - 1, coef_ref.shape[1])
    dy_ref[0:pads] = sent_ref[nz : nz + pads] * keep
    last = coef_ref[0, row] * lane_difference(dy_ref[inside]) + coef_ref[2, row] * (
        dy_ref[2:pads] - dy_ref[0:nz]
    )
    dy_ref[0:pads] = line_ref[...] * keep
    end = nz + pads
    extra = sent_ref[0:nz] - (
        sent_ref[end : end + 1] * lane_difference(dy_ref[inside])
        + sent_ref[end + 1 : end + 2] * (dy_ref[2:pads] - dy_ref[0:nz])
    )
    rhs_ref[...] = jnp.zeros_like(rhs_ref)
    for z in range(nz):
        rhs_ref[2 * z : 2 * z + 1] = extra[z : z + 1]
        rhs_ref[ny - 1 + 2 * z : ny + 2 * z] = last[z : z + 1]
    solved = product((ihigh_ref[...], ilow_ref[...]), split(rhs_ref[...]), NT)
    lane = lax.broadcasted_iota(jnp.int32, (half, width), 1)
    even = lane % 2 == 0
    lower = ((lane < ny // 2) & even) | ((lane >= ny // 2) & (lane < ny + ny // 2) & ~even)
    both = jnp.where(lower, solved[:half], pltpu.roll(solved[half:], ny, 1))
    ends = (lane % ny == 0) | (lane % ny == ny - 1)
    for z in range(nz):
        moved = pltpu.roll(both, width - 2 * z, 1) if z else both
        out_ref[:, z, :] = in_ref[:, z, :] + jnp.where(ends, moved, 0.0)


def patch(tiles, line, coefs, sent, inv_high, inv_low):
    half, nz, width = tiles.shape
    nx = 2 * half
    return pl.pallas_call(
        patch_kernel,
        in_specs=[VMEM] * 6,
        out_specs=VMEM,
        out_shape=pltpu.VMEM(tiles.shape, jnp.float32),
        scratch_shapes=[
            pltpu.VMEM((width, nx), jnp.float32),
            pltpu.VMEM((16, nx), jnp.float32),
        ],
        compiler_params=pltpu.CompilerParams(vmem_limit_bytes=16 * 1024 * 1024),
        cost_estimate=pl.CostEstimate(
            flops=6 * width * nx * nx, bytes_accessed=8 * half * nz * width, transcendentals=0
        ),
        name="patch",
    )(tiles, line, coefs, sent, inv_high, inv_low)


def plane_kernel(
    in_ref, zhigh_ref, zlow_ref, yhigh_ref, ylow_ref, out_ref, high_ref, low_ref
):
    slabs, blocks, depth, width = in_ref.shape
    half = width // 2
    rows = slabs * depth
    matz = zhigh_ref[...], zlow_ref[...]
    first = lax.broadcasted_iota(jnp.int32, (rows, width), 1) < half
    for b in range(0, blocks, 2):
        pair = []
        for k in (b, b + 1):
            pair.append(in_ref[:, k].reshape(rows, width))
        solved = product(matz, split(jnp.concatenate(pair, axis=1)), NN)
        left, right = solved[:, :width], solved[:, width:]
        columns = slice(b * half, (b + 2) * half)
        high_ref[:rows, columns], low_ref[:rows, columns] = split(
            jnp.where(first, left, pltpu.roll(right, half, 1))
        )
        high_ref[rows:, columns], low_ref[rows:, columns] = split(
            jnp.where(first, pltpu.roll(left, half, 1), right)
        )
    tile = (slabs, depth, width)
    for start in range(0, blocks, 4):
        columns = slice(start * half, (start + 4) * half)
        solved = product(
            (high_ref[...], low_ref[...]), (yhigh_ref[columns], ylow_ref[columns]), NT
        )
        for b in (start, start + 2):
            columns = slice((b - start) * half, (b - start + 2) * half)
            one, two = solved[:rows, columns], solved[rows:, columns]
            out_ref[:, b] = jnp.where(first, one, pltpu.roll(two, half, 1)).reshape(tile)
            out_ref[:, b + 1] = jnp.where(first, pltpu.roll(one, half, 1), two).reshape(tile)


def plane_solve(planes, *matrices):
    slabs, blocks, depth, width = planes.shape
    nz, ny = matrices[0].shape[0], matrices[-1].shape[0]
    return pl.pallas_call(
        plane_kernel,
        in_specs=[VMEM] * 5,
        out_specs=VMEM,
        out_shape=jax.ShapeDtypeStruct(planes.shape, jnp.float32),
        scratch_shapes=[pltpu.VMEM((2 * nz, ny), jnp.bfloat16)] * 2,
        compiler_params=pltpu.CompilerParams(vmem_limit_bytes=16 * 1024 * 1024),
        cost_estimate=pl.CostEstimate(
            flops=12 * nz * ny * (nz + ny), bytes_accessed=16 * nz * ny, transcendentals=0
        ),
        name="plane_solve",
    )(planes, *matrices)


def unpack_kernel(in_ref, out_ref, turned_ref, sems):
    sources, depth, width = in_ref.shape
    ny = width // 2
    copies = []
    for z in range(depth):
        turned = in_ref[:, z, :].T
        turned_ref[z, :, :sources] = turned[:ny]
        turned_ref[z, :, sources:] = turned[ny:]
        copies.append(pltpu.make_async_copy(turned_ref.at[z], out_ref.at[z], sems.at[z]))
        copies[-1].start()
    for copy in copies:
        copy.wait()


def unpack(tiles):
    sources, depth, width = tiles.shape
    shape = (depth, width // 2, 2 * sources)
    return pl.pallas_call(
        unpack_kernel,
        in_specs=[VMEM],
        out_specs=HBM,
        out_shape=jax.ShapeDtypeStruct(shape, jnp.float32),
        scratch_shapes=[pltpu.VMEM(shape, jnp.float32), pltpu.SemaphoreType.DMA((depth,))],
        cost_estimate=pl.CostEstimate(
            flops=0, bytes_accessed=8 * sources * depth * width, transcendentals=0
        ),
        name="unpack",
    )(pltpu.with_memory_space_constraint(tiles, pltpu.VMEM))


def swaps(axis, inner, outer):
    count = lax.axis_size(axis)

    def both(first):
        pairs = [(i, i + 1) for i in range(first, count - 1, 2)]
        return pairs + [(j, i) for i, j in pairs]

    return lax.ppermute(outer, axis, both(1)), lax.ppermute(inner, axis, both(0))


def shards(
    potential,
    fast_gate,
    slow_gate,
    tissue,
    region_ids,
    fibre_table,
    inverse_x,
    inverse_z,
    inverse_y,
):
    inner, outer = faces(potential)
    z_outer, z_inner = swaps("gz", inner, outer)
    held, excited, rows, coefs, inv_high, inv_low, *gates = ionic(
        fibre_table.T, potential, fast_gate, slow_gate, tissue, region_ids[0], inverse_x
    )
    z_outer, z_inner, rows, coefs = lax.optimization_barrier((z_outer, z_inner, rows, coefs))
    count = lax.axis_size("gy")
    sent = lax.ppermute(
        message(rows, coefs, z_inner, z_outer), "gy", [((i + 1) % count, i) for i in range(count)]
    )
    tiles, line, *matrices, new_fast, new_slow = stencil(
        held, excited, coefs, z_inner, z_outer, inv_high, inv_low, inverse_z, inverse_y, *gates
    )
    tiles = patch(tiles, line, coefs, sent, inv_high, inv_low)
    axes = ("gz", "gy")
    planes = lax.all_to_all(tiles, axes, split_axis=0, concat_axis=0, tiled=True)
    slabs, blocks = lax.axis_size("gz"), lax.axis_size("gy")
    solved = plane_solve(planes.reshape((slabs, blocks) + planes.shape[1:]), *matrices)
    back = lax.all_to_all(
        solved.reshape(planes.shape), axes, split_axis=0, concat_axis=0, tiled=True
    )
    return (unpack(back), new_fast, new_slow)


def solution(mesh):
    return jax.shard_map(
        shards,
        mesh=mesh,
        in_specs=(
            P("gz", "gy", None),
            P("gz", "gy", None),
            P("gz", "gy", None),
            P("gz", "gy", None),
            P("gz", "gy", None),
            P(),
            P(),
            P(),
            P(),
        ),
        out_specs=(P("gz", "gy", None), P("gz", "gy", None), P("gz", "gy", None)),
        check_vma=False,
    )
```

```python
import math

import jax
import jax.numpy as jnp
from jax import lax
from jax.experimental import pallas as pl
from jax.experimental.pallas import tpu as pltpu
from jax.sharding import PartitionSpec as P

time_step = 0.1
depol_tau = 0.25
repol_tau = 33.33
inward_tau = 29.0
outward_tau = 12.5
vclose_tau = 3.33
vopen_high = 19.6
vopen_low = 1250.0
wclose_tau = 870.0
wopen_tau = 41.0
gate_crit = 0.13
vgate_crit = 0.04
inward_crit = 0.85
inward_slope = 10.0

VMEM = pl.BlockSpec(memory_space=pltpu.VMEM)
HBM = pl.BlockSpec(memory_space=pltpu.HBM)
NT = (((1,), (1,)), ((), ()))
NN = (((1,), (0,)), ((), ()))


def decay(tau):
    return math.exp(-time_step / tau)


def split(values):
    high = values.astype(jnp.bfloat16)
    return high, (values - high.astype(jnp.float32)).astype(jnp.bfloat16)


def product(left, right, dims):
    (lh, ll), (rh, rl) = left, right

    def dot(a, b):
        return lax.dot_general(a, b, dims, preferred_element_type=jnp.float32)

    return dot(lh, rh) + (dot(lh, rl) + dot(ll, rh))


def pinned(*arrays):
    return [pltpu.with_memory_space_constraint(array, pltpu.HBM) for array in arrays]


def faces_kernel(pot_ref, inner_ref, outer_ref, sems):
    odd = lax.axis_index("gz") % 2
    last = pot_ref.shape[0] - 1
    copies = [
        pltpu.make_async_copy(pot_ref.at[last * (1 - odd)], inner_ref, sems.at[0]),
        pltpu.make_async_copy(pot_ref.at[last * odd], outer_ref, sems.at[1]),
    ]
    for copy in copies:
        copy.start()
    for copy in copies:
        copy.wait()


def faces(potential):
    plane = pltpu.VMEM(potential.shape[1:], jnp.float32)
    return pl.pallas_call(
        faces_kernel,
        in_specs=[HBM],
        out_specs=[VMEM] * 2,
        out_shape=[plane] * 2,
        scratch_shapes=[pltpu.SemaphoreType.DMA((2,))],
        name="faces",
    )(*pinned(potential))


def ionic_kernel(
    table_ref, pot_ref, fast_ref, slow_ref, tissue_ref, region_ref, inv_ref,
    potc_ref, exc_ref, rows_ref, coef_ref, ihigh_ref, ilow_ref, nfast_ref, nslow_ref,
    fast_v, slow_v, tissue_v, region_v, inv_v, table_s, in_sems, sems,
):
    nz, ny, nx = pot_ref.shape
    extra = [
        pltpu.make_async_copy(region_ref, region_v, sems.at[0]),
        pltpu.make_async_copy(inv_ref, inv_v, sems.at[1]),
        pltpu.make_async_copy(table_ref, table_s, sems.at[2]),
    ]
    pairs = ((pot_ref, potc_ref), (fast_ref, fast_v), (slow_ref, slow_v), (tissue_ref, tissue_v))
    loads = [
        [
            pltpu.make_async_copy(source.at[z], target.at[z], in_sems.at[k, z])
            for k, (source, target) in enumerate(pairs)
        ]
        for z in range(nz)
    ]
    for group in loads:
        for copy in group:
            copy.start()
    for copy in extra:
        copy.start()
    for z in range(nz):
        for copy in loads[z]:
            copy.wait()
        for row in range(0, ny, 8):
            rows = (z, slice(row, row + 8))
            p, v, w = potc_ref[rows], fast_v[rows], slow_v[rows]
            living = tissue_v[rows] == 1
            active = p >= gate_crit
            exc_ref[rows] = jnp.where(living, excite(p, v, w, active), p)
            target = jnp.where(active, 0.0, 1.0)
            keep_fast = jnp.where(
                active,
                decay(vclose_tau),
                jnp.where(p >= vgate_crit, decay(vopen_high), decay(vopen_low)),
            )
            keep_slow = jnp.where(active, decay(wclose_tau), decay(wopen_tau))
            nfast_ref[rows] = jnp.where(living, target + (v - target) * keep_fast, v)
            nslow_ref[rows] = jnp.where(living, target + (w - target) * keep_slow, w)
        for k, line in enumerate((potc_ref[z, 0:1], potc_ref[z, 1:2], exc_ref[z, 0:1])):
            rows_ref[k * nz + z : k * nz + z + 1] = line
    for copy in extra:
        copy.wait()
    for column, coef in enumerate(coefficients(table_s, region_v, nx)):
        coef_ref[column] = coef
    ihigh_ref[...], ilow_ref[...] = split(inv_v[...])


def ionic(table, potential, fast_gate, slow_gate, tissue, region, inverse_x):
    nz, ny, nx = potential.shape
    field = pltpu.VMEM((nz, ny, nx), jnp.float32)
    part = pltpu.VMEM((nx, nx), jnp.bfloat16)
    return pl.pallas_call(
        ionic_kernel,
        in_specs=[HBM] * 7,
        out_specs=[VMEM] * 8,
        out_shape=[
            field,
            field,
            pltpu.VMEM((3 * nz, nx), jnp.float32),
            pltpu.VMEM((3, ny // 8, nx), jnp.float32),
            part,
            part,
            field,
            field,
        ],
        scratch_shapes=[
            field,
            field,
            pltpu.VMEM((nz, ny, nx), jnp.int32),
            pltpu.VMEM(region.shape, jnp.int32),
            pltpu.VMEM((nx, nx), jnp.float32),
            pltpu.SMEM(table.shape, jnp.float32),
            pltpu.SemaphoreType.DMA((4, nz)),
            pltpu.SemaphoreType.DMA((3,)),
        ],
        compiler_params=pltpu.CompilerParams(vmem_limit_bytes=16 * 1024 * 1024),
        cost_estimate=pl.CostEstimate(
            flops=40 * nz * ny * nx, bytes_accessed=28 * nz * ny * nx, transcendentals=0
        ),
        name="ionic",
    )(*pinned(table, potential, fast_gate, slow_gate, tissue, region, inverse_x))


def excite(p, v, w, active):
    current = jnp.where(
        active,
        (1.0 / repol_tau) - v * (1.0 - p) * (p - gate_crit) * (1.0 / depol_tau),
        p * (1.0 / outward_tau),
    )
    current = current - w * (1.0 + jnp.tanh(inward_slope * (p - inward_crit))) * (
        1.0 / (2.0 * inward_tau)
    )
    return p - time_step * current


def lane_difference(values):
    width = values.shape[-1]
    lane = lax.broadcasted_iota(jnp.int32, values.shape, values.ndim - 1)
    ahead = pltpu.roll(values, width - 1, values.ndim - 1)
    behind = pltpu.roll(values, 1, values.ndim - 1)
    return jnp.where(lane == width - 1, 0.0, ahead) - jnp.where(lane == 0, 0.0, behind)


def coefficients(table_ref, region_ref, nx):
    blocks = region_ref.shape[1]
    spread = (
        lax.broadcasted_iota(jnp.int32, (blocks, nx), 1) // 8
        == lax.broadcasted_iota(jnp.int32, (blocks, nx), 0)
    ).astype(jnp.bfloat16)
    ids = lax.dot_general(
        region_ref[...].astype(jnp.float32).astype(jnp.bfloat16), spread, NN,
        preferred_element_type=jnp.float32,
    )
    coefs = []
    for column in range(3):
        coef = jnp.zeros_like(ids)
        for region in range(table_ref.shape[1]):
            coef = jnp.where(ids == float(region), 0.5 * table_ref[column, region], coef)
        coefs.append(coef)
    return coefs


def ordered(odd, inner, outer):
    return jnp.where(odd == 1, inner, outer), jnp.where(odd == 1, outer, inner)


def message_kernel(rows_ref, coef_ref, inner_ref, outer_ref, out_ref, pad_ref):
    nz = rows_ref.shape[0] // 3
    pads = nz + 2
    odd = lax.axis_index("gz") % 2
    for k in range(2):
        row = slice(k, k + 1)
        below, above = ordered(odd, inner_ref[row], outer_ref[row])
        pad_ref[k, 0:1] = below
        pad_ref[k, 1 : nz + 1] = rows_ref[k * nz : (k + 1) * nz]
        pad_ref[k, nz + 1 : pads] = above
    out_ref[0:nz] = rows_ref[2 * nz :] + (
        coef_ref[0, 0:1] * lane_difference(pad_ref[1, 1 : nz + 1])
        + coef_ref[1, 0:1] * lane_difference(pad_ref[0, 2:pads] - pad_ref[0, 0:nz])
        + coef_ref[2, 0:1] * (pad_ref[1, 2:pads] - pad_ref[1, 0:nz])
    )
    out_ref[nz : nz + pads] = pad_ref[0, 0:pads]
    out_ref[nz + pads : nz + pads + 1] = coef_ref[0, 0:1]
    out_ref[nz + pads + 1 : nz + pads + 2] = coef_ref[2, 0:1]
    rest = out_ref.shape[0] - (nz + pads + 2)
    out_ref[nz + pads + 2 :] = jnp.zeros((rest, out_ref.shape[1]), jnp.float32)


def message(rows, coefs, inner, outer):
    nz, nx = rows.shape[0] // 3, rows.shape[1]
    return pl.pallas_call(
        message_kernel,
        in_specs=[VMEM] * 4,
        out_specs=VMEM,
        out_shape=pltpu.VMEM((3 * nz, nx), jnp.float32),
        scratch_shapes=[pltpu.VMEM((2, 16, nx), jnp.float32)],
        compiler_params=pltpu.CompilerParams(vmem_limit_bytes=4 * 1024 * 1024),
        name="message",
    )(rows, coefs, inner, outer)


def stencil_kernel(
    pot_ref, exc_ref, coef_ref, inner_ref, outer_ref, ihigh_ref, ilow_ref, invz_ref, invy_ref,
    nfast_v, nslow_v,
    out_ref, line_ref, zhigh_ref, zlow_ref, yhigh_ref, ylow_ref, nfast_ref, nslow_ref,
    pad_ref, dy_ref, high_ref, low_ref, invz_v, invy_v, sems,
):
    nz, ny, nx = pot_ref.shape
    half = nx // 2
    loads = [
        pltpu.make_async_copy(invz_ref, invz_v, sems.at[0]),
        pltpu.make_async_copy(invy_ref, invy_v, sems.at[1]),
    ]
    stores = [
        pltpu.make_async_copy(nfast_v, nfast_ref, sems.at[2]),
        pltpu.make_async_copy(nslow_v, nslow_ref, sems.at[3]),
    ]
    for copy in loads + stores:
        copy.start()
    below, above = ordered(lax.axis_index("gz") % 2, inner_ref[...], outer_ref[...])
    nothing = jnp.zeros((1, nx), jnp.float32)
    for z in range(nz + 2):
        plane = below if z == 0 else above if z == nz + 1 else pot_ref[z - 1]
        pad_ref[z, 8 : 8 + ny] = plane
        pad_ref[z, 7:8] = nothing
        pad_ref[z, 8 + ny : 9 + ny] = nothing
        dy_ref[z] = pad_ref[z, 9 : 9 + ny] - pad_ref[z, 7 : 7 + ny]
        line_ref[z : z + 1] = plane[ny - 1 :]
    row = lax.broadcasted_iota(jnp.int32, (8, nx), 0)
    first = lax.broadcasted_iota(jnp.int32, (half, 2 * ny), 1) < ny
    matrix = ihigh_ref[...], ilow_ref[...]
    blocks = ny // 8
    for z in range(nz):
        parts = []
        for b in range(blocks):
            rows = slice(8 * b, 8 * b + 8)
            inside = slice(8 * b + 8, 8 * b + 16)
            mixed_xy = lane_difference(dy_ref[z + 1, rows])
            mixed_xz = lane_difference(pad_ref[z + 2, inside] - pad_ref[z, inside])
            mixed_yz = dy_ref[z + 2, rows] - dy_ref[z, rows]
            parts.append(
                exc_ref[z, rows]
                + (
                    coef_ref[0, b : b + 1] * mixed_xy
                    + coef_ref[1, b : b + 1] * mixed_xz
                    + coef_ref[2, b : b + 1] * mixed_yz
                )
            )
        parts[0] = jnp.where(row == 0, 0.0, parts[0])
        for b in range(0, blocks, 2):
            rows = slice(z * ny + 8 * b, z * ny + 8 * b + 16)
            high_ref[rows], low_ref[rows] = split(jnp.concatenate(parts[b : b + 2], axis=0))
        if z % 4 == 3:
            rows = slice((z - 3) * ny, (z + 1) * ny)
            solved = product(matrix, (high_ref[rows], low_ref[rows]), NT)
            for k in range(2):
                columns = slice(2 * k * ny, 2 * (k + 1) * ny)
                lower, upper = solved[:half, columns], solved[half:, columns]
                at = z - 3 + 2 * k
                out_ref[:, at, :] = jnp.where(first, lower, pltpu.roll(upper, ny, 1))
                out_ref[:, at + 1, :] = jnp.where(first, pltpu.roll(lower, ny, 1), upper)
    for copy in loads:
        copy.wait()
    zhigh_ref[...], zlow_ref[...] = split(invz_v[...])
    width = invy_v.shape[1]
    invy = invy_v[...]
    column = lax.broadcasted_iota(jnp.int32, invy.shape, 1)
    yhigh_ref[...], ylow_ref[...] = split(
        jnp.where(column % ny == 0, pltpu.roll(invy, width - ny, 1), invy)
    )
    for copy in stores:
        copy.wait()


def stencil(
    potential, excited, coefs, inner, outer, inv_high, inv_low, inverse_z, inverse_y, *gates
):
    nz, ny, nx = potential.shape
    return pl.pallas_call(
        stencil_kernel,
        in_specs=[VMEM] * 7 + [HBM] * 2 + [VMEM] * 2,
        out_specs=[VMEM] * 6 + [HBM] * 2,
        out_shape=[
            pltpu.VMEM((nx // 2, nz, 2 * ny), jnp.float32),
            pltpu.VMEM((nz + 2, nx), jnp.float32),
        ]
        + [pltpu.VMEM(inverse_z.shape, jnp.bfloat16)] * 2
        + [pltpu.VMEM(inverse_y.shape, jnp.bfloat16)] * 2
        + [jax.ShapeDtypeStruct((nz, ny, nx), jnp.float32)] * 2,
        scratch_shapes=[
            pltpu.VMEM((nz + 2, ny + 16, nx), jnp.float32),
            pltpu.VMEM((nz + 2, ny, nx), jnp.float32),
            pltpu.VMEM((nz * ny, nx), jnp.bfloat16),
            pltpu.VMEM((nz * ny, nx), jnp.bfloat16),
            pltpu.VMEM(inverse_z.shape, jnp.float32),
            pltpu.VMEM(inverse_y.shape, jnp.float32),
            pltpu.SemaphoreType.DMA((4,)),
        ],
        compiler_params=pltpu.CompilerParams(vmem_limit_bytes=24 * 1024 * 1024),
        cost_estimate=pl.CostEstimate(
            flops=6 * nz * ny * nx * nx, bytes_accessed=32 * nz * ny * nx, transcendentals=0
        ),
        name="stencil",
    )(
        potential, excited, coefs, inner, outer, inv_high, inv_low,
        *pinned(inverse_z, inverse_y), *gates,
    )


def patch_kernel(
    in_ref, line_ref, coef_ref, sent_ref, ihigh_ref, ilow_ref, out_ref, rhs_ref, dy_ref, both_ref
):
    half, nz, width = in_ref.shape
    ny = width // 2
    pads = nz + 2
    keep = jnp.where(lax.axis_index("gy") == lax.axis_size("gy") - 1, 0.0, 1.0)
    inside = slice(1, nz + 1)
    row = slice(coef_ref.shape[1] - 1, coef_ref.shape[1])
    dy_ref[0:pads] = sent_ref[nz : nz + pads] * keep
    last = coef_ref[0, row] * lane_difference(dy_ref[inside]) + coef_ref[2, row] * (
        dy_ref[2:pads] - dy_ref[0:nz]
    )
    dy_ref[0:pads] = line_ref[...] * keep
    end = nz + pads
    extra = sent_ref[0:nz] - (
        sent_ref[end : end + 1] * lane_difference(dy_ref[inside])
        + sent_ref[end + 1 : end + 2] * (dy_ref[2:pads] - dy_ref[0:nz])
    )
    rhs_ref[...] = jnp.zeros_like(rhs_ref)
    for z in range(nz):
        at = (width - 2 * z) % width
        rhs_ref[at : at + 1] = extra[z : z + 1]
        rhs_ref[ny - 1 - 2 * z : ny - 2 * z] = last[z : z + 1]
    high, low = split(rhs_ref[...])
    wide = lax.dot_general(
        ihigh_ref[...], jnp.concatenate([high, low], axis=0), NT, preferred_element_type=jnp.float32
    )
    solved = wide[:, :width] + (
        wide[:, width:]
        + lax.dot_general(ilow_ref[...], high, NT, preferred_element_type=jnp.float32)
    )
    lane = lax.broadcasted_iota(jnp.int32, (half, width), 1)
    quarter = ny // 2
    lower = ((lane < quarter) & (lane % 2 == 0)) | (
        (lane >= quarter) & (lane < ny + quarter) & (lane % 2 == 1)
    )
    lower = lower | ((lane >= ny + quarter) & (lane % 2 == 0))
    both_ref[...] = jnp.where(lower, solved[:half], pltpu.roll(solved[half:], ny, 1))
    lane = lax.broadcasted_iota(jnp.int32, (nz, width), 1)
    ends = (lane % ny == 0) | (lane % ny == ny - 1)
    for d in range(half):
        moved = pltpu.roll(
            jnp.broadcast_to(both_ref[d : d + 1], (nz, width)), 0, 1, stride=2, stride_axis=0
        )
        out_ref[d] = in_ref[d] + jnp.where(ends, moved, 0.0)


def patch(tiles, line, coefs, sent, inv_high, inv_low):
    half, nz, width = tiles.shape
    nx = 2 * half
    return pl.pallas_call(
        patch_kernel,
        in_specs=[VMEM] * 6,
        out_specs=VMEM,
        out_shape=pltpu.VMEM(tiles.shape, jnp.float32),
        scratch_shapes=[
            pltpu.VMEM((width, nx), jnp.float32),
            pltpu.VMEM((16, nx), jnp.float32),
            pltpu.VMEM((half, width), jnp.float32),
        ],
        compiler_params=pltpu.CompilerParams(vmem_limit_bytes=16 * 1024 * 1024),
        cost_estimate=pl.CostEstimate(
            flops=6 * width * nx * nx, bytes_accessed=8 * half * nz * width, transcendentals=0
        ),
        name="patch",
    )(tiles, line, coefs, sent, inv_high, inv_low)


def plane_kernel(
    in_ref, zhigh_ref, zlow_ref, yhigh_ref, ylow_ref, out_ref, high_ref, low_ref
):
    slabs, blocks, depth, width = in_ref.shape
    half = width // 2
    rows = slabs * depth
    matz = zhigh_ref[...], zlow_ref[...]
    first = lax.broadcasted_iota(jnp.int32, (rows, width), 1) < half
    for b in range(0, blocks, 2):
        pair = []
        for k in (b, b + 1):
            pair.append(in_ref[:, k].reshape(rows, width))
        solved = product(matz, split(jnp.concatenate(pair, axis=1)), NN)
        left, right = solved[:, :width], solved[:, width:]
        columns = slice(b * half, (b + 2) * half)
        high_ref[:rows, columns], low_ref[:rows, columns] = split(
            jnp.where(first, left, pltpu.roll(right, half, 1))
        )
        high_ref[rows:, columns], low_ref[rows:, columns] = split(
            jnp.where(first, pltpu.roll(left, half, 1), right)
        )
    tile = (slabs, depth, width)
    for start in range(0, blocks, 4):
        columns = slice(start * half, (start + 4) * half)
        solved = product(
            (high_ref[...], low_ref[...]), (yhigh_ref[columns], ylow_ref[columns]), NT
        )
        for b in (start, start + 2):
            columns = slice((b - start) * half, (b - start + 2) * half)
            one, two = solved[:rows, columns], solved[rows:, columns]
            out_ref[:, b] = jnp.where(first, one, pltpu.roll(two, half, 1)).reshape(tile)
            out_ref[:, b + 1] = jnp.where(first, pltpu.roll(one, half, 1), two).reshape(tile)


def plane_solve(planes, *matrices):
    slabs, blocks, depth, width = planes.shape
    nz, ny = matrices[0].shape[0], matrices[-1].shape[0]
    return pl.pallas_call(
        plane_kernel,
        in_specs=[VMEM] * 5,
        out_specs=VMEM,
        out_shape=jax.ShapeDtypeStruct(planes.shape, jnp.float32),
        scratch_shapes=[pltpu.VMEM((2 * nz, ny), jnp.bfloat16)] * 2,
        compiler_params=pltpu.CompilerParams(vmem_limit_bytes=16 * 1024 * 1024),
        cost_estimate=pl.CostEstimate(
            flops=12 * nz * ny * (nz + ny), bytes_accessed=16 * nz * ny, transcendentals=0
        ),
        name="plane_solve",
    )(planes, *matrices)


def unpack_kernel(in_ref, out_ref, turned_ref, sems):
    sources, depth, width = in_ref.shape
    ny = width // 2
    copies = []
    turned = jnp.transpose(in_ref[...], (1, 2, 0))
    for z in range(depth):
        turned_ref[z, :, :sources] = turned[z, :ny]
        turned_ref[z, :, sources:] = turned[z, ny:]
        copies.append(pltpu.make_async_copy(turned_ref.at[z], out_ref.at[z], sems.at[z]))
        copies[-1].start()
    for copy in copies:
        copy.wait()


def unpack(tiles):
    sources, depth, width = tiles.shape
    shape = (depth, width // 2, 2 * sources)
    return pl.pallas_call(
        unpack_kernel,
        in_specs=[VMEM],
        out_specs=HBM,
        out_shape=jax.ShapeDtypeStruct(shape, jnp.float32),
        scratch_shapes=[pltpu.VMEM(shape, jnp.float32), pltpu.SemaphoreType.DMA((depth,))],
        cost_estimate=pl.CostEstimate(
            flops=0, bytes_accessed=8 * sources * depth * width, transcendentals=0
        ),
        name="unpack",
    )(pltpu.with_memory_space_constraint(tiles, pltpu.VMEM))


def swaps(axis, inner, outer):
    count = lax.axis_size(axis)

    def both(first):
        pairs = [(i, i + 1) for i in range(first, count - 1, 2)]
        return pairs + [(j, i) for i, j in pairs]

    return lax.ppermute(outer, axis, both(1)), lax.ppermute(inner, axis, both(0))


def shards(
    potential,
    fast_gate,
    slow_gate,
    tissue,
    region_ids,
    fibre_table,
    inverse_x,
    inverse_z,
    inverse_y,
):
    inner, outer = faces(potential)
    z_outer, z_inner = swaps("gz", inner, outer)
    held, excited, rows, coefs, inv_high, inv_low, *gates = ionic(
        fibre_table.T, potential, fast_gate, slow_gate, tissue, region_ids[0], inverse_x
    )
    z_outer, z_inner, rows, coefs = lax.optimization_barrier((z_outer, z_inner, rows, coefs))
    count = lax.axis_size("gy")
    sent = lax.ppermute(
        message(rows, coefs, z_inner, z_outer), "gy", [((i + 1) % count, i) for i in range(count)]
    )
    tiles, line, *matrices, new_fast, new_slow = stencil(
        held, excited, coefs, z_inner, z_outer, inv_high, inv_low, inverse_z, inverse_y, *gates
    )
    tiles = patch(tiles, line, coefs, sent, inv_high, inv_low)
    axes = ("gz", "gy")
    planes = lax.all_to_all(tiles, axes, split_axis=0, concat_axis=0, tiled=True)
    slabs, blocks = lax.axis_size("gz"), lax.axis_size("gy")
    solved = plane_solve(planes.reshape((slabs, blocks) + planes.shape[1:]), *matrices)
    back = lax.all_to_all(
        solved.reshape(planes.shape), axes, split_axis=0, concat_axis=0, tiled=True
    )
    return (unpack(back), new_fast, new_slow)


def solution(mesh):
    return jax.shard_map(
        shards,
        mesh=mesh,
        in_specs=(
            P("gz", "gy", None),
            P("gz", "gy", None),
            P("gz", "gy", None),
            P("gz", "gy", None),
            P("gz", "gy", None),
            P(),
            P(),
            P(),
            P(),
        ),
        out_specs=(P("gz", "gy", None), P("gz", "gy", None), P("gz", "gy", None)),
        check_vma=False,
    )
```

```python
import math

import jax
import jax.numpy as jnp
from jax import lax
from jax.experimental import pallas as pl
from jax.experimental.pallas import tpu as pltpu
from jax.sharding import PartitionSpec as P

time_step = 0.1
depol_tau = 0.25
repol_tau = 33.33
inward_tau = 29.0
outward_tau = 12.5
vclose_tau = 3.33
vopen_high = 19.6
vopen_low = 1250.0
wclose_tau = 870.0
wopen_tau = 41.0
gate_crit = 0.13
vgate_crit = 0.04
inward_crit = 0.85
inward_slope = 10.0

VMEM = pl.BlockSpec(memory_space=pltpu.VMEM)
HBM = pl.BlockSpec(memory_space=pltpu.HBM)
NT = (((1,), (1,)), ((), ()))
NN = (((1,), (0,)), ((), ()))


def decay(tau):
    return math.exp(-time_step / tau)


def split(values):
    high = values.astype(jnp.bfloat16)
    return high, (values - high.astype(jnp.float32)).astype(jnp.bfloat16)


def product(left, right, dims):
    (lh, ll), (rh, rl) = left, right

    def dot(a, b):
        return lax.dot_general(a, b, dims, preferred_element_type=jnp.float32)

    return dot(lh, rh) + (dot(lh, rl) + dot(ll, rh))


def pinned(*arrays):
    return [pltpu.with_memory_space_constraint(array, pltpu.HBM) for array in arrays]


def faces_kernel(pot_ref, inner_ref, outer_ref, sems):
    odd = lax.axis_index("gz") % 2
    last = pot_ref.shape[0] - 1
    copies = [
        pltpu.make_async_copy(pot_ref.at[last * (1 - odd)], inner_ref, sems.at[0]),
        pltpu.make_async_copy(pot_ref.at[last * odd], outer_ref, sems.at[1]),
    ]
    for copy in copies:
        copy.start()
    for copy in copies:
        copy.wait()


def faces(potential):
    plane = pltpu.VMEM(potential.shape[1:], jnp.float32)
    return pl.pallas_call(
        faces_kernel,
        in_specs=[HBM],
        out_specs=[VMEM] * 2,
        out_shape=[plane] * 2,
        scratch_shapes=[pltpu.SemaphoreType.DMA((2,))],
        name="faces",
    )(*pinned(potential))


def ionic_kernel(
    table_ref, pot_ref, fast_ref, slow_ref, tissue_ref, region_ref, inv_ref,
    potc_ref, exc_ref, rows_ref, coef_ref, ihigh_ref, ilow_ref, nfast_ref, nslow_ref,
    fast_v, slow_v, tissue_v, region_v, inv_v, table_s, in_sems, sems,
):
    nz, ny, nx = pot_ref.shape
    extra = [
        pltpu.make_async_copy(region_ref, region_v, sems.at[0]),
        pltpu.make_async_copy(inv_ref, inv_v, sems.at[1]),
        pltpu.make_async_copy(table_ref, table_s, sems.at[2]),
    ]
    pairs = ((pot_ref, potc_ref), (fast_ref, fast_v), (slow_ref, slow_v), (tissue_ref, tissue_v))
    loads = [
        [
            pltpu.make_async_copy(source.at[z], target.at[z], in_sems.at[k, z])
            for k, (source, target) in enumerate(pairs)
        ]
        for z in range(nz)
    ]
    for group in loads:
        for copy in group:
            copy.start()
    for copy in extra:
        copy.start()
    for z in range(nz):
        for copy in loads[z]:
            copy.wait()
        for row in range(0, ny, 8):
            rows = (z, slice(row, row + 8))
            p, v, w = potc_ref[rows], fast_v[rows], slow_v[rows]
            living = tissue_v[rows] == 1
            active = p >= gate_crit
            exc_ref[rows] = jnp.where(living, excite(p, v, w, active), p)
            target = jnp.where(active, 0.0, 1.0)
            keep_fast = jnp.where(
                active,
                decay(vclose_tau),
                jnp.where(p >= vgate_crit, decay(vopen_high), decay(vopen_low)),
            )
            keep_slow = jnp.where(active, decay(wclose_tau), decay(wopen_tau))
            nfast_ref[rows] = jnp.where(living, target + (v - target) * keep_fast, v)
            nslow_ref[rows] = jnp.where(living, target + (w - target) * keep_slow, w)
        for k, line in enumerate(
            (potc_ref[z, ny - 1 :], potc_ref[z, ny - 2 : ny - 1], exc_ref[z, ny - 1 :])
        ):
            rows_ref[k * nz + z : k * nz + z + 1] = line
    for copy in extra:
        copy.wait()
    for column, coef in enumerate(coefficients(table_s, region_v, nx)):
        coef_ref[column] = coef
    ihigh_ref[...], ilow_ref[...] = split(inv_v[...])


def ionic(table, potential, fast_gate, slow_gate, tissue, region, inverse_x):
    nz, ny, nx = potential.shape
    field = pltpu.VMEM((nz, ny, nx), jnp.float32)
    part = pltpu.VMEM((nx, nx), jnp.bfloat16)
    return pl.pallas_call(
        ionic_kernel,
        in_specs=[HBM] * 7,
        out_specs=[VMEM] * 8,
        out_shape=[
            field,
            field,
            pltpu.VMEM((3 * nz, nx), jnp.float32),
            pltpu.VMEM((3, ny // 8, nx), jnp.float32),
            part,
            part,
            field,
            field,
        ],
        scratch_shapes=[
            field,
            field,
            pltpu.VMEM((nz, ny, nx), jnp.int32),
            pltpu.VMEM(region.shape, jnp.int32),
            pltpu.VMEM((nx, nx), jnp.float32),
            pltpu.SMEM(table.shape, jnp.float32),
            pltpu.SemaphoreType.DMA((4, nz)),
            pltpu.SemaphoreType.DMA((3,)),
        ],
        compiler_params=pltpu.CompilerParams(vmem_limit_bytes=16 * 1024 * 1024),
        cost_estimate=pl.CostEstimate(
            flops=40 * nz * ny * nx, bytes_accessed=28 * nz * ny * nx, transcendentals=0
        ),
        name="ionic",
    )(*pinned(table, potential, fast_gate, slow_gate, tissue, region, inverse_x))


def excite(p, v, w, active):
    current = jnp.where(
        active,
        (1.0 / repol_tau) - v * (1.0 - p) * (p - gate_crit) * (1.0 / depol_tau),
        p * (1.0 / outward_tau),
    )
    current = current - w * (1.0 + jnp.tanh(inward_slope * (p - inward_crit))) * (
        1.0 / (2.0 * inward_tau)
    )
    return p - time_step * current


def lane_difference(values):
    width = values.shape[-1]
    lane = lax.broadcasted_iota(jnp.int32, values.shape, values.ndim - 1)
    ahead = pltpu.roll(values, width - 1, values.ndim - 1)
    behind = pltpu.roll(values, 1, values.ndim - 1)
    return jnp.where(lane == width - 1, 0.0, ahead) - jnp.where(lane == 0, 0.0, behind)


def coefficients(table_ref, region_ref, nx):
    blocks = region_ref.shape[1]
    spread = (
        lax.broadcasted_iota(jnp.int32, (blocks, nx), 1) // 8
        == lax.broadcasted_iota(jnp.int32, (blocks, nx), 0)
    ).astype(jnp.bfloat16)
    ids = lax.dot_general(
        region_ref[...].astype(jnp.float32).astype(jnp.bfloat16), spread, NN,
        preferred_element_type=jnp.float32,
    )
    coefs = []
    for column in range(3):
        coef = jnp.zeros_like(ids)
        for region in range(table_ref.shape[1]):
            coef = jnp.where(ids == float(region), 0.5 * table_ref[column, region], coef)
        coefs.append(coef)
    return coefs


def ordered(odd, inner, outer):
    return jnp.where(odd == 1, inner, outer), jnp.where(odd == 1, outer, inner)


def message_kernel(rows_ref, coef_ref, inner_ref, outer_ref, out_ref, pad_ref):
    nz = rows_ref.shape[0] // 3
    pads = nz + 2
    ny = inner_ref.shape[0]
    block = slice(coef_ref.shape[1] - 1, coef_ref.shape[1])
    odd = lax.axis_index("gz") % 2
    for k in range(2):
        row = slice(ny - 1 - k, ny - k)
        below, above = ordered(odd, inner_ref[row], outer_ref[row])
        pad_ref[k, 0:1] = below
        pad_ref[k, 1 : nz + 1] = rows_ref[k * nz : (k + 1) * nz]
        pad_ref[k, nz + 1 : pads] = above
    out_ref[0:nz] = rows_ref[2 * nz :] + (
        coef_ref[1, block] * lane_difference(pad_ref[0, 2:pads] - pad_ref[0, 0:nz])
        - coef_ref[0, block] * lane_difference(pad_ref[1, 1 : nz + 1])
        - coef_ref[2, block] * (pad_ref[1, 2:pads] - pad_ref[1, 0:nz])
    )
    out_ref[nz : nz + pads] = pad_ref[0, 0:pads]
    out_ref[nz + pads : nz + pads + 1] = coef_ref[0, block]
    out_ref[nz + pads + 1 : nz + pads + 2] = coef_ref[2, block]
    rest = out_ref.shape[0] - (nz + pads + 2)
    out_ref[nz + pads + 2 :] = jnp.zeros((rest, out_ref.shape[1]), jnp.float32)


def message(rows, coefs, inner, outer):
    nz, nx = rows.shape[0] // 3, rows.shape[1]
    return pl.pallas_call(
        message_kernel,
        in_specs=[VMEM] * 4,
        out_specs=VMEM,
        out_shape=pltpu.VMEM((3 * nz, nx), jnp.float32),
        scratch_shapes=[pltpu.VMEM((2, 16, nx), jnp.float32)],
        compiler_params=pltpu.CompilerParams(vmem_limit_bytes=4 * 1024 * 1024),
        name="message",
    )(rows, coefs, inner, outer)


def stencil_kernel(
    pot_ref, exc_ref, coef_ref, inner_ref, outer_ref, ihigh_ref, ilow_ref, invz_ref, invy_ref,
    nfast_v, nslow_v,
    out_ref, line_ref, zhigh_ref, zlow_ref, yhigh_ref, ylow_ref, nfast_ref, nslow_ref,
    pad_ref, dy_ref, high_ref, low_ref, invz_v, invy_v, sems,
):
    nz, ny, nx = pot_ref.shape
    half = nx // 2
    loads = [
        pltpu.make_async_copy(invz_ref, invz_v, sems.at[0]),
        pltpu.make_async_copy(invy_ref, invy_v, sems.at[1]),
    ]
    stores = [
        pltpu.make_async_copy(nfast_v, nfast_ref, sems.at[2]),
        pltpu.make_async_copy(nslow_v, nslow_ref, sems.at[3]),
    ]
    for copy in loads + stores:
        copy.start()
    below, above = ordered(lax.axis_index("gz") % 2, inner_ref[...], outer_ref[...])
    nothing = jnp.zeros((1, nx), jnp.float32)
    for z in range(nz + 2):
        plane = below if z == 0 else above if z == nz + 1 else pot_ref[z - 1]
        pad_ref[z, 8 : 8 + ny] = plane
        pad_ref[z, 7:8] = nothing
        pad_ref[z, 8 + ny : 9 + ny] = nothing
        dy_ref[z] = pad_ref[z, 9 : 9 + ny] - pad_ref[z, 7 : 7 + ny]
        line_ref[z : z + 1] = plane[0:1]
    row = lax.broadcasted_iota(jnp.int32, (8, nx), 0)
    first = lax.broadcasted_iota(jnp.int32, (half, 2 * ny), 1) < ny
    matrix = ihigh_ref[...], ilow_ref[...]
    blocks = ny // 8
    for z in range(nz):
        parts = []
        for b in range(blocks):
            rows = slice(8 * b, 8 * b + 8)
            inside = slice(8 * b + 8, 8 * b + 16)
            mixed_xy = lane_difference(dy_ref[z + 1, rows])
            mixed_xz = lane_difference(pad_ref[z + 2, inside] - pad_ref[z, inside])
            mixed_yz = dy_ref[z + 2, rows] - dy_ref[z, rows]
            parts.append(
                exc_ref[z, rows]
                + (
                    coef_ref[0, b : b + 1] * mixed_xy
                    + coef_ref[1, b : b + 1] * mixed_xz
                    + coef_ref[2, b : b + 1] * mixed_yz
                )
            )
        parts[-1] = jnp.where(row == 7, 0.0, parts[-1])
        for b in range(0, blocks, 2):
            rows = slice(z * ny + 8 * b, z * ny + 8 * b + 16)
            high_ref[rows], low_ref[rows] = split(jnp.concatenate(parts[b : b + 2], axis=0))
        if z % 4 == 3:
            rows = slice((z - 3) * ny, (z + 1) * ny)
            solved = product(matrix, (high_ref[rows], low_ref[rows]), NT)
            for k in range(2):
                columns = slice(2 * k * ny, 2 * (k + 1) * ny)
                lower, upper = solved[:half, columns], solved[half:, columns]
                at = z - 3 + 2 * k
                out_ref[:, at, :] = jnp.where(first, lower, pltpu.roll(upper, ny, 1))
                out_ref[:, at + 1, :] = jnp.where(first, pltpu.roll(lower, ny, 1), upper)
    for copy in loads:
        copy.wait()
    zhigh_ref[...], zlow_ref[...] = split(invz_v[...])
    invy = invy_v[...]
    column = lax.broadcasted_iota(jnp.int32, invy.shape, 1)
    yhigh_ref[...], ylow_ref[...] = split(
        jnp.where(column % ny == ny - 1, pltpu.roll(invy, ny, 1), invy)
    )
    for copy in stores:
        copy.wait()


def stencil(
    potential, excited, coefs, inner, outer, inv_high, inv_low, inverse_z, inverse_y, *gates
):
    nz, ny, nx = potential.shape
    return pl.pallas_call(
        stencil_kernel,
        in_specs=[VMEM] * 7 + [HBM] * 2 + [VMEM] * 2,
        out_specs=[VMEM] * 6 + [HBM] * 2,
        out_shape=[
            pltpu.VMEM((nx // 2, nz, 2 * ny), jnp.float32),
            pltpu.VMEM((nz + 2, nx), jnp.float32),
        ]
        + [pltpu.VMEM(inverse_z.shape, jnp.bfloat16)] * 2
        + [pltpu.VMEM(inverse_y.shape, jnp.bfloat16)] * 2
        + [jax.ShapeDtypeStruct((nz, ny, nx), jnp.float32)] * 2,
        scratch_shapes=[
            pltpu.VMEM((nz + 2, ny + 16, nx), jnp.float32),
            pltpu.VMEM((nz + 2, ny, nx), jnp.float32),
            pltpu.VMEM((nz * ny, nx), jnp.bfloat16),
            pltpu.VMEM((nz * ny, nx), jnp.bfloat16),
            pltpu.VMEM(inverse_z.shape, jnp.float32),
            pltpu.VMEM(inverse_y.shape, jnp.float32),
            pltpu.SemaphoreType.DMA((4,)),
        ],
        compiler_params=pltpu.CompilerParams(vmem_limit_bytes=24 * 1024 * 1024),
        cost_estimate=pl.CostEstimate(
            flops=6 * nz * ny * nx * nx, bytes_accessed=32 * nz * ny * nx, transcendentals=0
        ),
        name="stencil",
    )(
        potential, excited, coefs, inner, outer, inv_high, inv_low,
        *pinned(inverse_z, inverse_y), *gates,
    )


def patch_kernel(
    in_ref, line_ref, coef_ref, sent_ref, ihigh_ref, ilow_ref, out_ref, rhs_ref, dy_ref, both_ref
):
    half, nz, width = in_ref.shape
    ny = width // 2
    pads = nz + 2
    keep = jnp.where(lax.axis_index("gy") == 0, 0.0, 1.0)
    inside = slice(1, nz + 1)
    dy_ref[0:pads] = sent_ref[nz : nz + pads] * -keep
    first = coef_ref[0, 0:1] * lane_difference(dy_ref[inside]) + coef_ref[2, 0:1] * (
        dy_ref[2:pads] - dy_ref[0:nz]
    )
    dy_ref[0:pads] = line_ref[...] * keep
    end = nz + pads
    extra = sent_ref[0:nz] + (
        sent_ref[end : end + 1] * lane_difference(dy_ref[inside])
        + sent_ref[end + 1 : end + 2] * (dy_ref[2:pads] - dy_ref[0:nz])
    )
    rhs_ref[...] = jnp.zeros_like(rhs_ref)
    for z in range(nz):
        at = (width - 2 * z) % width
        rhs_ref[at : at + 1] = first[z : z + 1]
        rhs_ref[ny - 1 - 2 * z : ny - 2 * z] = extra[z : z + 1]
    high, low = split(rhs_ref[...])
    wide = lax.dot_general(
        ihigh_ref[...], jnp.concatenate([high, low], axis=0), NT, preferred_element_type=jnp.float32
    )
    solved = wide[:, :width] + (
        wide[:, width:]
        + lax.dot_general(ilow_ref[...], high, NT, preferred_element_type=jnp.float32)
    )
    lane = lax.broadcasted_iota(jnp.int32, (half, width), 1)
    quarter = ny // 2
    lower = ((lane < quarter) & (lane % 2 == 0)) | (
        (lane >= quarter) & (lane < ny + quarter) & (lane % 2 == 1)
    )
    lower = lower | ((lane >= ny + quarter) & (lane % 2 == 0))
    both_ref[...] = jnp.where(lower, solved[:half], pltpu.roll(solved[half:], ny, 1))
    lane = lax.broadcasted_iota(jnp.int32, (nz, width), 1)
    ends = (lane % ny == 0) | (lane % ny == ny - 1)
    for d in range(half):
        moved = pltpu.roll(
            jnp.broadcast_to(both_ref[d : d + 1], (nz, width)), 0, 1, stride=2, stride_axis=0
        )
        out_ref[d] = in_ref[d] + jnp.where(ends, moved, 0.0)


def patch(tiles, line, coefs, sent, inv_high, inv_low):
    half, nz, width = tiles.shape
    nx = 2 * half
    return pl.pallas_call(
        patch_kernel,
        in_specs=[VMEM] * 6,
        out_specs=VMEM,
        out_shape=pltpu.VMEM(tiles.shape, jnp.float32),
        scratch_shapes=[
            pltpu.VMEM((width, nx), jnp.float32),
            pltpu.VMEM((16, nx), jnp.float32),
            pltpu.VMEM((half, width), jnp.float32),
        ],
        compiler_params=pltpu.CompilerParams(vmem_limit_bytes=16 * 1024 * 1024),
        cost_estimate=pl.CostEstimate(
            flops=6 * width * nx * nx, bytes_accessed=8 * half * nz * width, transcendentals=0
        ),
        name="patch",
    )(tiles, line, coefs, sent, inv_high, inv_low)


def plane_kernel(
    in_ref, zhigh_ref, zlow_ref, yhigh_ref, ylow_ref, out_ref, high_ref, low_ref
):
    slabs, blocks, depth, width = in_ref.shape
    half = width // 2
    rows = slabs * depth
    matz = zhigh_ref[...], zlow_ref[...]
    first = lax.broadcasted_iota(jnp.int32, (rows, width), 1) < half
    for b in range(0, blocks, 2):
        pair = []
        for k in (b, b + 1):
            pair.append(in_ref[:, k].reshape(rows, width))
        solved = product(matz, split(jnp.concatenate(pair, axis=1)), NN)
        left, right = solved[:, :width], solved[:, width:]
        columns = slice(b * half, (b + 2) * half)
        high_ref[:rows, columns], low_ref[:rows, columns] = split(
            jnp.where(first, left, pltpu.roll(right, half, 1))
        )
        high_ref[rows:, columns], low_ref[rows:, columns] = split(
            jnp.where(first, pltpu.roll(left, half, 1), right)
        )
    tile = (slabs, depth, width)
    for start in range(0, blocks, 4):
        columns = slice(start * half, (start + 4) * half)
        solved = product(
            (high_ref[...], low_ref[...]), (yhigh_ref[columns], ylow_ref[columns]), NT
        )
        for b in (start, start + 2):
            columns = slice((b - start) * half, (b - start + 2) * half)
            one, two = solved[:rows, columns], solved[rows:, columns]
            out_ref[:, b] = jnp.where(first, one, pltpu.roll(two, half, 1)).reshape(tile)
            out_ref[:, b + 1] = jnp.where(first, pltpu.roll(one, half, 1), two).reshape(tile)


def plane_solve(planes, *matrices):
    slabs, blocks, depth, width = planes.shape
    nz, ny = matrices[0].shape[0], matrices[-1].shape[0]
    return pl.pallas_call(
        plane_kernel,
        in_specs=[VMEM] * 5,
        out_specs=VMEM,
        out_shape=jax.ShapeDtypeStruct(planes.shape, jnp.float32),
        scratch_shapes=[pltpu.VMEM((2 * nz, ny), jnp.bfloat16)] * 2,
        compiler_params=pltpu.CompilerParams(vmem_limit_bytes=16 * 1024 * 1024),
        cost_estimate=pl.CostEstimate(
            flops=12 * nz * ny * (nz + ny), bytes_accessed=16 * nz * ny, transcendentals=0
        ),
        name="plane_solve",
    )(planes, *matrices)


def unpack_kernel(in_ref, out_ref, turned_ref, sems):
    sources, depth, width = in_ref.shape
    ny = width // 2
    copies = []
    turned = jnp.transpose(in_ref[...], (1, 2, 0))
    for z in range(depth):
        turned_ref[z, :, :sources] = turned[z, :ny]
        turned_ref[z, :, sources:] = turned[z, ny:]
        copies.append(pltpu.make_async_copy(turned_ref.at[z], out_ref.at[z], sems.at[z]))
        copies[-1].start()
    for copy in copies:
        copy.wait()


def unpack(tiles):
    sources, depth, width = tiles.shape
    shape = (depth, width // 2, 2 * sources)
    return pl.pallas_call(
        unpack_kernel,
        in_specs=[VMEM],
        out_specs=HBM,
        out_shape=jax.ShapeDtypeStruct(shape, jnp.float32),
        scratch_shapes=[pltpu.VMEM(shape, jnp.float32), pltpu.SemaphoreType.DMA((depth,))],
        cost_estimate=pl.CostEstimate(
            flops=0, bytes_accessed=8 * sources * depth * width, transcendentals=0
        ),
        name="unpack",
    )(pltpu.with_memory_space_constraint(tiles, pltpu.VMEM))


def swaps(axis, inner, outer):
    count = lax.axis_size(axis)

    def both(first):
        pairs = [(i, i + 1) for i in range(first, count - 1, 2)]
        return pairs + [(j, i) for i, j in pairs]

    return lax.ppermute(outer, axis, both(1)), lax.ppermute(inner, axis, both(0))


def shards(
    potential,
    fast_gate,
    slow_gate,
    tissue,
    region_ids,
    fibre_table,
    inverse_x,
    inverse_z,
    inverse_y,
):
    inner, outer = faces(potential)
    z_outer, z_inner = swaps("gz", inner, outer)
    held, excited, rows, coefs, inv_high, inv_low, *gates = ionic(
        fibre_table.T, potential, fast_gate, slow_gate, tissue, region_ids[0], inverse_x
    )
    z_outer, z_inner, rows, coefs = lax.optimization_barrier((z_outer, z_inner, rows, coefs))
    count = lax.axis_size("gy")
    sent = lax.ppermute(
        message(rows, coefs, z_inner, z_outer), "gy", [(i, (i + 1) % count) for i in range(count)]
    )
    tiles, line, *matrices, new_fast, new_slow = stencil(
        held, excited, coefs, z_inner, z_outer, inv_high, inv_low, inverse_z, inverse_y, *gates
    )
    tiles = patch(tiles, line, coefs, sent, inv_high, inv_low)
    axes = ("gz", "gy")
    planes = lax.all_to_all(tiles, axes, split_axis=0, concat_axis=0, tiled=True)
    slabs, blocks = lax.axis_size("gz"), lax.axis_size("gy")
    solved = plane_solve(planes.reshape((slabs, blocks) + planes.shape[1:]), *matrices)
    back = lax.all_to_all(
        solved.reshape(planes.shape), axes, split_axis=0, concat_axis=0, tiled=True
    )
    return (unpack(back), new_fast, new_slow)


def solution(mesh):
    return jax.shard_map(
        shards,
        mesh=mesh,
        in_specs=(
            P("gz", "gy", None),
            P("gz", "gy", None),
            P("gz", "gy", None),
            P("gz", "gy", None),
            P("gz", "gy", None),
            P(),
            P(),
            P(),
            P(),
        ),
        out_specs=(P("gz", "gy", None), P("gz", "gy", None), P("gz", "gy", None)),
        check_vma=False,
    )
```

```python
import math

import jax
import jax.numpy as jnp
from jax import lax
from jax.experimental import pallas as pl
from jax.experimental.pallas import tpu as pltpu
from jax.sharding import PartitionSpec as P

time_step = 0.1
depol_tau = 0.25
repol_tau = 33.33
inward_tau = 29.0
outward_tau = 12.5
vclose_tau = 3.33
vopen_high = 19.6
vopen_low = 1250.0
wclose_tau = 870.0
wopen_tau = 41.0
gate_crit = 0.13
vgate_crit = 0.04
inward_crit = 0.85
inward_slope = 10.0

VMEM = pl.BlockSpec(memory_space=pltpu.VMEM)
HBM = pl.BlockSpec(memory_space=pltpu.HBM)
NT = (((1,), (1,)), ((), ()))
NN = (((1,), (0,)), ((), ()))


def decay(tau):
    return math.exp(-time_step / tau)


def split(values):
    high = values.astype(jnp.bfloat16)
    return high, (values - high.astype(jnp.float32)).astype(jnp.bfloat16)


def product(left, right, dims):
    (lh, ll), (rh, rl) = left, right

    def dot(a, b):
        return lax.dot_general(a, b, dims, preferred_element_type=jnp.float32)

    return dot(lh, rh) + (dot(lh, rl) + dot(ll, rh))


def pinned(*arrays):
    return [pltpu.with_memory_space_constraint(array, pltpu.HBM) for array in arrays]


def faces_kernel(pot_ref, inner_ref, outer_ref, sems):
    odd = lax.axis_index("gz") % 2
    last = pot_ref.shape[0] - 1
    copies = [
        pltpu.make_async_copy(pot_ref.at[last * (1 - odd)], inner_ref, sems.at[0]),
        pltpu.make_async_copy(pot_ref.at[last * odd], outer_ref, sems.at[1]),
    ]
    for copy in copies:
        copy.start()
    for copy in copies:
        copy.wait()


def faces(potential):
    plane = pltpu.VMEM(potential.shape[1:], jnp.float32)
    return pl.pallas_call(
        faces_kernel,
        in_specs=[HBM],
        out_specs=[VMEM] * 2,
        out_shape=[plane] * 2,
        scratch_shapes=[pltpu.SemaphoreType.DMA((2,))],
        name="faces",
    )(*pinned(potential))


def ionic_kernel(
    table_ref, pot_ref, fast_ref, slow_ref, tissue_ref, region_ref, inv_ref,
    potc_ref, exc_ref, rows_ref, coef_ref, ihigh_ref, ilow_ref, nfast_ref, nslow_ref,
    fast_v, slow_v, tissue_v, region_v, inv_v, table_s, in_sems, sems,
):
    nz, ny, nx = pot_ref.shape
    extra = [
        pltpu.make_async_copy(region_ref, region_v, sems.at[0]),
        pltpu.make_async_copy(inv_ref, inv_v, sems.at[1]),
        pltpu.make_async_copy(table_ref, table_s, sems.at[2]),
    ]
    pairs = ((pot_ref, potc_ref), (fast_ref, fast_v), (slow_ref, slow_v), (tissue_ref, tissue_v))
    loads = [
        [
            pltpu.make_async_copy(source.at[z], target.at[z], in_sems.at[k, z])
            for k, (source, target) in enumerate(pairs)
        ]
        for z in range(nz)
    ]
    for group in loads:
        for copy in group:
            copy.start()
    for copy in extra:
        copy.start()
    for z in range(nz):
        for copy in loads[z]:
            copy.wait()
        for row in range(0, ny, 8):
            rows = (z, slice(row, row + 8))
            p, v, w = potc_ref[rows], fast_v[rows], slow_v[rows]
            living = tissue_v[rows] == 1
            active = p >= gate_crit
            exc_ref[rows] = jnp.where(living, excite(p, v, w, active), p)
            target = jnp.where(active, 0.0, 1.0)
            keep_fast = jnp.where(
                active,
                decay(vclose_tau),
                jnp.where(p >= vgate_crit, decay(vopen_high), decay(vopen_low)),
            )
            keep_slow = jnp.where(active, decay(wclose_tau), decay(wopen_tau))
            nfast_ref[rows] = jnp.where(living, target + (v - target) * keep_fast, v)
            nslow_ref[rows] = jnp.where(living, target + (w - target) * keep_slow, w)
        for k, line in enumerate(
            (potc_ref[z, ny - 1 :], potc_ref[z, ny - 2 : ny - 1], exc_ref[z, ny - 1 :])
        ):
            rows_ref[k * nz + z : k * nz + z + 1] = line
    for copy in extra:
        copy.wait()
    for column, coef in enumerate(coefficients(table_s, region_v, nx)):
        coef_ref[column] = coef
    ihigh_ref[...], ilow_ref[...] = split(inv_v[...])


def ionic(table, potential, fast_gate, slow_gate, tissue, region, inverse_x):
    nz, ny, nx = potential.shape
    field = pltpu.VMEM((nz, ny, nx), jnp.float32)
    part = pltpu.VMEM((nx, nx), jnp.bfloat16)
    return pl.pallas_call(
        ionic_kernel,
        in_specs=[HBM] * 7,
        out_specs=[VMEM] * 8,
        out_shape=[
            field,
            field,
            pltpu.VMEM((3 * nz, nx), jnp.float32),
            pltpu.VMEM((3, ny // 8, nx), jnp.float32),
            part,
            part,
            field,
            field,
        ],
        scratch_shapes=[
            field,
            field,
            pltpu.VMEM((nz, ny, nx), jnp.int32),
            pltpu.VMEM(region.shape, jnp.int32),
            pltpu.VMEM((nx, nx), jnp.float32),
            pltpu.SMEM(table.shape, jnp.float32),
            pltpu.SemaphoreType.DMA((4, nz)),
            pltpu.SemaphoreType.DMA((3,)),
        ],
        compiler_params=pltpu.CompilerParams(vmem_limit_bytes=16 * 1024 * 1024),
        cost_estimate=pl.CostEstimate(
            flops=40 * nz * ny * nx, bytes_accessed=28 * nz * ny * nx, transcendentals=0
        ),
        name="ionic",
    )(*pinned(table, potential, fast_gate, slow_gate, tissue, region, inverse_x))


def excite(p, v, w, active):
    current = jnp.where(
        active,
        (1.0 / repol_tau) - v * (1.0 - p) * (p - gate_crit) * (1.0 / depol_tau),
        p * (1.0 / outward_tau),
    )
    current = current - w * (1.0 + jnp.tanh(inward_slope * (p - inward_crit))) * (
        1.0 / (2.0 * inward_tau)
    )
    return p - time_step * current


def lane_difference(values):
    width = values.shape[-1]
    lane = lax.broadcasted_iota(jnp.int32, values.shape, values.ndim - 1)
    ahead = pltpu.roll(values, width - 1, values.ndim - 1)
    behind = pltpu.roll(values, 1, values.ndim - 1)
    return jnp.where(lane == width - 1, 0.0, ahead) - jnp.where(lane == 0, 0.0, behind)


def coefficients(table_ref, region_ref, nx):
    blocks = region_ref.shape[1]
    spread = (
        lax.broadcasted_iota(jnp.int32, (blocks, nx), 1) // 8
        == lax.broadcasted_iota(jnp.int32, (blocks, nx), 0)
    ).astype(jnp.bfloat16)
    ids = lax.dot_general(
        region_ref[...].astype(jnp.float32).astype(jnp.bfloat16), spread, NN,
        preferred_element_type=jnp.float32,
    )
    coefs = []
    for column in range(3):
        coef = jnp.zeros_like(ids)
        for region in range(table_ref.shape[1]):
            coef = jnp.where(ids == float(region), 0.5 * table_ref[column, region], coef)
        coefs.append(coef)
    return coefs


def ordered(odd, inner, outer):
    return jnp.where(odd == 1, inner, outer), jnp.where(odd == 1, outer, inner)


def message_kernel(rows_ref, coef_ref, inner_ref, outer_ref, out_ref, pad_ref):
    nz = rows_ref.shape[0] // 3
    pads = nz + 2
    ny = inner_ref.shape[0]
    block = slice(coef_ref.shape[1] - 1, coef_ref.shape[1])
    odd = lax.axis_index("gz") % 2
    for k in range(2):
        row = slice(ny - 1 - k, ny - k)
        below, above = ordered(odd, inner_ref[row], outer_ref[row])
        pad_ref[k, 0:1] = below
        pad_ref[k, 1 : nz + 1] = rows_ref[k * nz : (k + 1) * nz]
        pad_ref[k, nz + 1 : pads] = above
    partial = rows_ref[2 * nz :] + (
        coef_ref[1, block] * lane_difference(pad_ref[0, 2:pads] - pad_ref[0, 0:nz])
        - coef_ref[0, block] * lane_difference(pad_ref[1, 1 : nz + 1])
        - coef_ref[2, block] * (pad_ref[1, 2:pads] - pad_ref[1, 0:nz])
    )
    lines = nz + pads + 2
    parts = ((0, partial), (nz, pad_ref[0, 0:pads]))
    parts += ((nz + pads, coef_ref[0, block]), (nz + pads + 1, coef_ref[2, block]))
    for start, part in parts:
        for k in range(part.shape[1] // 128):
            at = k * lines + start
            out_ref[at : at + part.shape[0]] = part[:, 128 * k : 128 * (k + 1)]


def message(rows, coefs, inner, outer):
    nz, nx = rows.shape[0] // 3, rows.shape[1]
    return pl.pallas_call(
        message_kernel,
        in_specs=[VMEM] * 4,
        out_specs=VMEM,
        out_shape=pltpu.VMEM(((2 * nz + 4) * nx // 128, 128), jnp.float32),
        scratch_shapes=[pltpu.VMEM((2, 16, nx), jnp.float32)],
        compiler_params=pltpu.CompilerParams(vmem_limit_bytes=4 * 1024 * 1024),
        name="message",
    )(rows, coefs, inner, outer)


def stencil_kernel(
    pot_ref, exc_ref, coef_ref, inner_ref, outer_ref, ihigh_ref, ilow_ref, invz_ref, invy_ref,
    nfast_v, nslow_v,
    out_ref, line_ref, zhigh_ref, zlow_ref, yhigh_ref, ylow_ref, nfast_ref, nslow_ref,
    pad_ref, dy_ref, high_ref, low_ref, invz_v, invy_v, sems,
):
    nz, ny, nx = pot_ref.shape
    half = nx // 2
    loads = [
        pltpu.make_async_copy(invz_ref, invz_v, sems.at[0]),
        pltpu.make_async_copy(invy_ref, invy_v, sems.at[1]),
    ]
    stores = [
        pltpu.make_async_copy(nfast_v, nfast_ref, sems.at[2]),
        pltpu.make_async_copy(nslow_v, nslow_ref, sems.at[3]),
    ]
    for copy in loads + stores:
        copy.start()
    below, above = ordered(lax.axis_index("gz") % 2, inner_ref[...], outer_ref[...])
    nothing = jnp.zeros((1, nx), jnp.float32)
    for z in range(nz + 2):
        plane = below if z == 0 else above if z == nz + 1 else pot_ref[z - 1]
        pad_ref[z, 8 : 8 + ny] = plane
        pad_ref[z, 7:8] = nothing
        pad_ref[z, 8 + ny : 9 + ny] = nothing
        dy_ref[z] = pad_ref[z, 9 : 9 + ny] - pad_ref[z, 7 : 7 + ny]
        line_ref[z : z + 1] = plane[0:1]
    row = lax.broadcasted_iota(jnp.int32, (8, nx), 0)
    first = lax.broadcasted_iota(jnp.int32, (half, 2 * ny), 1) < ny
    matrix = ihigh_ref[...], ilow_ref[...]
    blocks = ny // 8
    for z in range(nz):
        parts = []
        for b in range(blocks):
            rows = slice(8 * b, 8 * b + 8)
            inside = slice(8 * b + 8, 8 * b + 16)
            mixed_xy = lane_difference(dy_ref[z + 1, rows])
            mixed_xz = lane_difference(pad_ref[z + 2, inside] - pad_ref[z, inside])
            mixed_yz = dy_ref[z + 2, rows] - dy_ref[z, rows]
            parts.append(
                exc_ref[z, rows]
                + (
                    coef_ref[0, b : b + 1] * mixed_xy
                    + coef_ref[1, b : b + 1] * mixed_xz
                    + coef_ref[2, b : b + 1] * mixed_yz
                )
            )
        parts[-1] = jnp.where(row == 7, 0.0, parts[-1])
        for b in range(0, blocks, 2):
            rows = slice(z * ny + 8 * b, z * ny + 8 * b + 16)
            high_ref[rows], low_ref[rows] = split(jnp.concatenate(parts[b : b + 2], axis=0))
        if z % 4 == 3:
            rows = slice((z - 3) * ny, (z + 1) * ny)
            solved = product(matrix, (high_ref[rows], low_ref[rows]), NT)
            for k in range(2):
                columns = slice(2 * k * ny, 2 * (k + 1) * ny)
                lower, upper = solved[:half, columns], solved[half:, columns]
                at = z - 3 + 2 * k
                out_ref[:, at, :] = jnp.where(first, lower, pltpu.roll(upper, ny, 1))
                out_ref[:, at + 1, :] = jnp.where(first, pltpu.roll(lower, ny, 1), upper)
    for copy in loads:
        copy.wait()
    zhigh_ref[...], zlow_ref[...] = split(invz_v[...])
    invy = invy_v[...]
    column = lax.broadcasted_iota(jnp.int32, invy.shape, 1)
    yhigh_ref[...], ylow_ref[...] = split(
        jnp.where(column % ny == ny - 1, pltpu.roll(invy, ny, 1), invy)
    )
    for copy in stores:
        copy.wait()


def stencil(
    potential, excited, coefs, inner, outer, inv_high, inv_low, inverse_z, inverse_y, *gates
):
    nz, ny, nx = potential.shape
    return pl.pallas_call(
        stencil_kernel,
        in_specs=[VMEM] * 7 + [HBM] * 2 + [VMEM] * 2,
        out_specs=[VMEM] * 6 + [HBM] * 2,
        out_shape=[
            pltpu.VMEM((nx // 2, nz, 2 * ny), jnp.float32),
            pltpu.VMEM((nz + 2, nx), jnp.float32),
        ]
        + [pltpu.VMEM(inverse_z.shape, jnp.bfloat16)] * 2
        + [pltpu.VMEM(inverse_y.shape, jnp.bfloat16)] * 2
        + [jax.ShapeDtypeStruct((nz, ny, nx), jnp.float32)] * 2,
        scratch_shapes=[
            pltpu.VMEM((nz + 2, ny + 16, nx), jnp.float32),
            pltpu.VMEM((nz + 2, ny, nx), jnp.float32),
            pltpu.VMEM((nz * ny, nx), jnp.bfloat16),
            pltpu.VMEM((nz * ny, nx), jnp.bfloat16),
            pltpu.VMEM(inverse_z.shape, jnp.float32),
            pltpu.VMEM(inverse_y.shape, jnp.float32),
            pltpu.SemaphoreType.DMA((4,)),
        ],
        compiler_params=pltpu.CompilerParams(vmem_limit_bytes=24 * 1024 * 1024),
        cost_estimate=pl.CostEstimate(
            flops=6 * nz * ny * nx * nx, bytes_accessed=32 * nz * ny * nx, transcendentals=0
        ),
        name="stencil",
    )(
        potential, excited, coefs, inner, outer, inv_high, inv_low,
        *pinned(inverse_z, inverse_y), *gates,
    )


def patch_kernel(
    in_ref, line_ref, coef_ref, packed_ref, ihigh_ref, ilow_ref,
    out_ref, rhs_ref, dy_ref, both_ref, sent_ref,
):
    half, nz, width = in_ref.shape
    ny = width // 2
    pads = nz + 2
    keep = jnp.where(lax.axis_index("gy") == 0, 0.0, 1.0)
    lines = nz + pads + 2
    for k in range(packed_ref.shape[0] // lines):
        sent_ref[0:lines, 128 * k : 128 * (k + 1)] = packed_ref[k * lines : (k + 1) * lines]
    inside = slice(1, nz + 1)
    dy_ref[0:pads] = sent_ref[nz : nz + pads] * -keep
    first = coef_ref[0, 0:1] * lane_difference(dy_ref[inside]) + coef_ref[2, 0:1] * (
        dy_ref[2:pads] - dy_ref[0:nz]
    )
    dy_ref[0:pads] = line_ref[...] * keep
    end = nz + pads
    extra = sent_ref[0:nz] + (
        sent_ref[end : end + 1] * lane_difference(dy_ref[inside])
        + sent_ref[end + 1 : end + 2] * (dy_ref[2:pads] - dy_ref[0:nz])
    )
    rhs_ref[...] = jnp.zeros_like(rhs_ref)
    for z in range(nz):
        at = (width - 2 * z) % width
        rhs_ref[at : at + 1] = first[z : z + 1]
        rhs_ref[ny - 1 - 2 * z : ny - 2 * z] = extra[z : z + 1]
    high, low = split(rhs_ref[...])
    wide = lax.dot_general(
        ihigh_ref[...], jnp.concatenate([high, low], axis=0), NT, preferred_element_type=jnp.float32
    )
    solved = wide[:, :width] + (
        wide[:, width:]
        + lax.dot_general(ilow_ref[...], high, NT, preferred_element_type=jnp.float32)
    )
    lane = lax.broadcasted_iota(jnp.int32, (half, width), 1)
    quarter = ny // 2
    lower = ((lane < quarter) & (lane % 2 == 0)) | (
        (lane >= quarter) & (lane < ny + quarter) & (lane % 2 == 1)
    )
    lower = lower | ((lane >= ny + quarter) & (lane % 2 == 0))
    both_ref[...] = jnp.where(lower, solved[:half], pltpu.roll(solved[half:], ny, 1))
    lane = lax.broadcasted_iota(jnp.int32, (nz, width), 1)
    ends = (lane % ny == 0) | (lane % ny == ny - 1)
    for d in range(half):
        moved = pltpu.roll(
            jnp.broadcast_to(both_ref[d : d + 1], (nz, width)), 0, 1, stride=2, stride_axis=0
        )
        out_ref[d] = in_ref[d] + jnp.where(ends, moved, 0.0)


def patch(tiles, line, coefs, sent, inv_high, inv_low):
    half, nz, width = tiles.shape
    nx = 2 * half
    return pl.pallas_call(
        patch_kernel,
        in_specs=[VMEM] * 6,
        out_specs=VMEM,
        out_shape=pltpu.VMEM(tiles.shape, jnp.float32),
        scratch_shapes=[
            pltpu.VMEM((width, nx), jnp.float32),
            pltpu.VMEM((16, nx), jnp.float32),
            pltpu.VMEM((half, width), jnp.float32),
            pltpu.VMEM((3 * nz, nx), jnp.float32),
        ],
        compiler_params=pltpu.CompilerParams(vmem_limit_bytes=16 * 1024 * 1024),
        cost_estimate=pl.CostEstimate(
            flops=6 * width * nx * nx, bytes_accessed=8 * half * nz * width, transcendentals=0
        ),
        name="patch",
    )(tiles, line, coefs, sent, inv_high, inv_low)


def plane_kernel(
    in_ref, zhigh_ref, zlow_ref, yhigh_ref, ylow_ref, out_ref, high_ref, low_ref
):
    slabs, blocks, depth, width = in_ref.shape
    half = width // 2
    rows = slabs * depth
    matz = zhigh_ref[...], zlow_ref[...]
    first = lax.broadcasted_iota(jnp.int32, (rows, width), 1) < half
    for b in range(0, blocks, 2):
        pair = []
        for k in (b, b + 1):
            pair.append(in_ref[:, k].reshape(rows, width))
        solved = product(matz, split(jnp.concatenate(pair, axis=1)), NN)
        left, right = solved[:, :width], solved[:, width:]
        columns = slice(b * half, (b + 2) * half)
        high_ref[:rows, columns], low_ref[:rows, columns] = split(
            jnp.where(first, left, pltpu.roll(right, half, 1))
        )
        high_ref[rows:, columns], low_ref[rows:, columns] = split(
            jnp.where(first, pltpu.roll(left, half, 1), right)
        )
    tile = (slabs, depth, width)
    for start in range(0, blocks, 4):
        columns = slice(start * half, (start + 4) * half)
        solved = product(
            (high_ref[...], low_ref[...]), (yhigh_ref[columns], ylow_ref[columns]), NT
        )
        for b in (start, start + 2):
            columns = slice((b - start) * half, (b - start + 2) * half)
            one, two = solved[:rows, columns], solved[rows:, columns]
            out_ref[:, b] = jnp.where(first, one, pltpu.roll(two, half, 1)).reshape(tile)
            out_ref[:, b + 1] = jnp.where(first, pltpu.roll(one, half, 1), two).reshape(tile)


def plane_solve(planes, *matrices):
    slabs, blocks, depth, width = planes.shape
    nz, ny = matrices[0].shape[0], matrices[-1].shape[0]
    return pl.pallas_call(
        plane_kernel,
        in_specs=[VMEM] * 5,
        out_specs=VMEM,
        out_shape=jax.ShapeDtypeStruct(planes.shape, jnp.float32),
        scratch_shapes=[pltpu.VMEM((2 * nz, ny), jnp.bfloat16)] * 2,
        compiler_params=pltpu.CompilerParams(vmem_limit_bytes=16 * 1024 * 1024),
        cost_estimate=pl.CostEstimate(
            flops=12 * nz * ny * (nz + ny), bytes_accessed=16 * nz * ny, transcendentals=0
        ),
        name="plane_solve",
    )(planes, *matrices)


def unpack_kernel(in_ref, out_ref, turned_ref, sems):
    sources, depth, width = in_ref.shape
    ny = width // 2
    copies = []
    turned = jnp.transpose(in_ref[...], (1, 2, 0))
    for z in range(depth):
        turned_ref[z, :, :sources] = turned[z, :ny]
        turned_ref[z, :, sources:] = turned[z, ny:]
        copies.append(pltpu.make_async_copy(turned_ref.at[z], out_ref.at[z], sems.at[z]))
        copies[-1].start()
    for copy in copies:
        copy.wait()


def unpack(tiles):
    sources, depth, width = tiles.shape
    shape = (depth, width // 2, 2 * sources)
    return pl.pallas_call(
        unpack_kernel,
        in_specs=[VMEM],
        out_specs=HBM,
        out_shape=jax.ShapeDtypeStruct(shape, jnp.float32),
        scratch_shapes=[pltpu.VMEM(shape, jnp.float32), pltpu.SemaphoreType.DMA((depth,))],
        cost_estimate=pl.CostEstimate(
            flops=0, bytes_accessed=8 * sources * depth * width, transcendentals=0
        ),
        name="unpack",
    )(pltpu.with_memory_space_constraint(tiles, pltpu.VMEM))


def swaps(axis, inner, outer):
    count = lax.axis_size(axis)

    def both(first):
        pairs = [(i, i + 1) for i in range(first, count - 1, 2)]
        return pairs + [(j, i) for i, j in pairs]

    return lax.ppermute(outer, axis, both(1)), lax.ppermute(inner, axis, both(0))


def shards(
    potential,
    fast_gate,
    slow_gate,
    tissue,
    region_ids,
    fibre_table,
    inverse_x,
    inverse_z,
    inverse_y,
):
    inner, outer = faces(potential)
    z_outer, z_inner = swaps("gz", inner, outer)
    held, excited, rows, coefs, inv_high, inv_low, *gates = ionic(
        fibre_table.T, potential, fast_gate, slow_gate, tissue, region_ids[0], inverse_x
    )
    z_outer, z_inner, rows, coefs = lax.optimization_barrier((z_outer, z_inner, rows, coefs))
    count = lax.axis_size("gy")
    sent = lax.ppermute(
        message(rows, coefs, z_inner, z_outer), "gy", [(i, (i + 1) % count) for i in range(count)]
    )
    tiles, line, *matrices, new_fast, new_slow = stencil(
        held, excited, coefs, z_inner, z_outer, inv_high, inv_low, inverse_z, inverse_y, *gates
    )
    tiles = patch(tiles, line, coefs, sent, inv_high, inv_low)
    axes = ("gz", "gy")
    planes = lax.all_to_all(tiles, axes, split_axis=0, concat_axis=0, tiled=True)
    slabs, blocks = lax.axis_size("gz"), lax.axis_size("gy")
    solved = plane_solve(planes.reshape((slabs, blocks) + planes.shape[1:]), *matrices)
    back = lax.all_to_all(
        solved.reshape(planes.shape), axes, split_axis=0, concat_axis=0, tiled=True
    )
    return (unpack(back), new_fast, new_slow)


def solution(mesh):
    return jax.shard_map(
        shards,
        mesh=mesh,
        in_specs=(
            P("gz", "gy", None),
            P("gz", "gy", None),
            P("gz", "gy", None),
            P("gz", "gy", None),
            P("gz", "gy", None),
            P(),
            P(),
            P(),
            P(),
        ),
        out_specs=(P("gz", "gy", None), P("gz", "gy", None), P("gz", "gy", None)),
        check_vma=False,
    )
```
